256 devices in a mesh: context: 32 (over y, z), tensor: 8 (over x, core).
Axes of the slice: x: 4, y: 4, z: 8, core: 2. Of those that a mesh axis runs over, the one named last changes fastest.
Arguments:
- stream_rows: bfloat16 [9216, 7168], P('context', 'tensor'), may hold values from -3 to 3
- picks: int32 [9216], P('context'), may hold values from 0 to 1536, as said below
- router: float32 [9216], P('context'), may hold values from 0.25 to 2
- queries: bfloat16 [9216, 4096], P('context', 'tensor'), may hold values from -100 to 100
- keys: bfloat16 [9216, 1024], P('context', 'tensor'), may hold values from -6 to 6
- values: bfloat16 [9216, 1024], P('context', 'tensor'), may hold values from -6 to 6
- out_weight: bfloat16 [4096, 7168], P('tensor'), may hold values from -0.09375 to 0.09375
Outputs:
- updated: bfloat16 [9216, 7168], P('context', 'tensor')
The draws below stay inside these ranges and needn't reach their ends.
Inputs may be any that keep to these rules, and one draw needn't show every extreme that they name: `picks`: each block of 288 slots (one index of context) holds distinct local token indices in increasing order followed by entries equal to 1536; a block has 96 to 288 picked tokens, and some block has exactly 288.
All inputs are finite; a program needn't handle non-finite values.
Results may differ from the reference program's by a relative error of at most 0.012.
Values may be sent and summed in bfloat16 or wider, within the bound.
A program may use at most 64 MiB of HBM per device.

```python
import math
import jax
import jax.numpy as jnp
from jax import lax

D = 7168
HEADS = 32
KV_HEADS = 8
HD = 128
TOK_DEV = 1536
CAP = 288
SLOTS = 9216
TOKENS = 49152
N_CONTEXT = 32
N_TENSOR = 8


def draw_picks(key, part):
    own_key = jax.random.fold_in(key, 5)
    count_key, full_key, perm_key = jax.random.split(own_key, 3)
    counts = jax.random.randint(count_key, (N_CONTEXT,), CAP // 3, CAP + 1)
    full_shard = jax.random.randint(full_key, (), 0, N_CONTEXT)
    counts = jnp.where(jnp.arange(N_CONTEXT) == full_shard, CAP, counts)

    def one_shard(shard_idx, shard_count):
        order = jax.random.permutation(jax.random.fold_in(perm_key, shard_idx), TOK_DEV)[:CAP]
        chosen = jnp.where(jnp.arange(CAP) < shard_count, order, TOK_DEV)
        return jnp.sort(chosen)
    table = jax.vmap(one_shard)(jnp.arange(N_CONTEXT), counts)
    return table.reshape(SLOTS).astype(jnp.int32)


def draw_queries(key, part):
    own_key = jax.random.fold_in(key, 7)
    group_size = HEADS // KV_HEADS
    noise = jnp.clip(jax.random.normal(own_key, (SLOTS, KV_HEADS, group_size, HD)) * 1.5, -9.0, 9.0)
    return noise.reshape(SLOTS, HEADS * HD).astype(jnp.bfloat16)


def draw_keys(key, part):
    own_key = jax.random.fold_in(key, 9)
    noise = jnp.clip(jax.random.normal(own_key, (SLOTS, KV_HEADS, HD)), -6.0, 6.0)
    return noise.reshape(SLOTS, KV_HEADS * HD).astype(jnp.bfloat16)


def steps_of(stream_key, dims, cuts, low, top_value):
    loudness, own = 1.0, jax.random.fold_in(stream_key, 6)
    for dim, shards_of in cuts:
        heights = jnp.exp(jax.random.uniform(jax.random.fold_in(own, dim), (shards_of,), jnp.float32, low / len(cuts), top_value / len(cuts)))
        loudness = loudness * jnp.repeat(heights, dims[dim] // shards_of).reshape([-1 if axis == dim else 1 for axis in range(len(dims))])
    return loudness


def gaussian(key, shape, deviation, limit, cuts=(), kind=jnp.bfloat16):
    result = jax.random.normal(key, shape, jnp.float32) * deviation
    if len(cuts) > 0:
        result = steps_of(key, shape, cuts, -0.22, 0.18) * result
    return jnp.clip(result, min=-limit, max=limit).astype(kind)


def setup_inputs(seed: int = 0) -> dict:
    key_list = jax.random.split(jax.random.key(seed), 8)
    return {
        "stream_rows": gaussian(key_list[0], (SLOTS, D), 0.5, 3.0, ((0, 32), (1, 8))),
        "picks": draw_picks(jax.random.fold_in(key_list[7], 71), 0),
        "router": jnp.clip(jnp.exp(math.log(2.0) - 2.0794415 * jax.random.uniform(key_list[2], (SLOTS,), jnp.float32) ** steps_of(key_list[2], (SLOTS,), ((0, 32),), -0.2, 0.2)), 0.25, 2.0),
        "queries": draw_queries(jax.random.fold_in(key_list[7], 71), 0),
        "keys": draw_keys(jax.random.fold_in(key_list[7], 71), 0),
        "values": gaussian(key_list[5], (SLOTS, KV_HEADS * HD), 1.0, 6.0, ((0, 32), (1, 8))),
        "out_weight": gaussian(key_list[6], (HEADS * HD, D), (HEADS * HD) ** -0.5, 0.09375, ((0, 8),)),
    }


NEG_FILL = -1e30


def reference(stream_rows, picks, router, queries, keys, values, out_weight):
    slot_ids = jnp.arange(SLOTS, dtype=jnp.int32)
    is_valid = picks < TOK_DEV
    global_pos = (slot_ids // CAP) * TOK_DEV + picks
    key_pos = jnp.where(is_valid, global_pos, TOKENS).astype(jnp.int32)
    query_pos = jnp.where(is_valid, global_pos, -1).astype(jnp.int32)
    group_size = HEADS // KV_HEADS
    score_scale = HD ** -0.5
    key_all = keys.astype(jnp.float32).reshape(SLOTS, KV_HEADS, HD)
    value_all = values.astype(jnp.float32).reshape(SLOTS, KV_HEADS, HD)
    query_blocks = queries.astype(jnp.float32).reshape(N_CONTEXT, CAP, KV_HEADS, group_size, HD)

    def attend(block_args):
        query_block, positions = block_args
        scores = jnp.einsum("qkgd,skd->kgqs", query_block, key_all) * score_scale
        visible = key_pos[None, :] <= positions[:, None]
        scores = jnp.where(visible[None, None], scores, NEG_FILL)
        row_max = jnp.max(scores, axis=-1, keepdims=True)
        weights = jnp.exp(scores - row_max)
        row_total = jnp.sum(weights, axis=-1)
        rounded = lax.optimization_barrier(weights.astype(jnp.bfloat16)).astype(jnp.float32)
        mixed_out = jnp.einsum("kgqs,skd->qkgd", rounded, value_all)
        mixed_out = mixed_out / jnp.transpose(row_total, (2, 0, 1))[..., None]
        return mixed_out.reshape(CAP, HEADS * HD).astype(jnp.bfloat16)

    attended = lax.map(attend, (query_blocks, query_pos.reshape(N_CONTEXT, CAP)))
    attended = attended.reshape(SLOTS, HEADS * HD)
    head_cols = HEADS * HD // N_TENSOR
    projected = jnp.zeros((SLOTS, D), jnp.float32)
    for tensor_idx in range(N_TENSOR):
        partial_value = jnp.dot(attended[:, tensor_idx * head_cols:(tensor_idx + 1) * head_cols],
                          out_weight[tensor_idx * head_cols:(tensor_idx + 1) * head_cols],
                          preferred_element_type=jnp.float32)
        projected = projected + lax.optimization_barrier(partial_value.astype(jnp.bfloat16)).astype(jnp.float32)
    residual = stream_rows.astype(jnp.float32)
    updated = jnp.where(is_valid[:, None], residual + router[:, None] * projected, residual)
    return updated.astype(jnp.bfloat16)
```

```python
import jax
import jax.numpy as jnp
from jax import lax
from jax.experimental import pallas as pl
from jax.experimental.pallas import tpu as pltpu
from jax.sharding import PartitionSpec as P

MESH = pl.DeviceIdType.MESH

TOK_DEV = 1536
CAP = 288
HD = 128
NY, NZ, NX = 4, 8, 4
WIDTH = 896
GROUP = 4
KAPPA = 128**-0.5 * 1.4426950408889634
NEG = -1e30
FILL = 64.0
TILE = 144

ROWS = {"A": 160, "B": 128}
FIRST = {"A": 0, "B": 160}
TURNS = {"A": (4, 3), "B0": (3, 4), "Bm": (4, 3), "Bp": (3, 4), "B2": (4, 3)}
ROW_OF = {"A": 0, "B0": 0, "Bm": 3, "Bp": 1, "B2": 2}
OFFSETS = (0, -1, -2, -3, 4, 1, 2, 3)
UPWARDS = (0, -1, -2, -3)

ORDER = (
    ("c", "diag", 0), ("c", "diag", 1),
    ("w", "YB", "P"), ("w", "YB", "M"), ("w", "ZR", "A", 1), ("w", "ZL", "A", 1), ("w", "YP", 0), ("w", "YM", 0),
    ("w", "ZR", "B0", 1), ("w", "ZL", "B0", 1), ("w", "YB", "2"), ("w", "ZL", "Bp", 1), ("w", "ZR", "A", 2),
    ("w", "YM", -1), ("w", "YP", -1), ("w", "ZR", "Bp", 1), ("w", "ZL", "A", 2), ("w", "YM", 1), ("w", "ZR", "B0", 2),
    ("w", "ZL", "B0", 2), ("w", "YP", 1), ("w", "YM", -2), ("w", "ZL", "Bp", 2), ("w", "ZR", "A", 3), ("w", "YP2", 0),
    ("w", "YM", 2), ("w", "ZR", "Bp", 2), ("w", "ZL", "A", 3), ("w", "YP", -2), ("w", "YM2", 1), ("w", "ZR", "B0", 3),
    ("w", "ZL", "B0", 3), ("w", "YP2", -1), ("w", "ZL", "Bp", 3), ("w", "YM", -3), ("w", "ZR", "A", 4),
    ("c", "A", 0, 0), ("w", "YP", 2), ("w", "ZL", "B0", 4), ("c", "A", 0, 1), ("w", "YM2", 2), ("w", "ZR", "Bp", 3),
    ("c", "B", 0, 0), ("w", "ZL", "Bp", 4), ("w", "YP", -3), ("w", "ZR", "Bm", 1), ("w", "YM", 3), ("c", "B", 0, 1),
    ("w", "ZL", "Bm", 1), ("c", "B", 1, 0), ("w", "ZR", "B2", 1), ("w", "YP", 3), ("w", "YM", 4), ("c", "B", 1, 1),
    ("w", "ZL", "B2", 1), ("w", "ZR", "Bm", 2), ("c", "A", 1, 0), ("w", "YP2", -2), ("w", "YM2", 3), ("w", "ZL", "Bm", 2),
    ("c", "A", 1, 1), ("w", "ZR", "B2", 2), ("w", "YP", 4), ("c", "A", 3, 0), ("w", "YM2", 4), ("w", "ZL", "B2", 2),
    ("w", "ZR", "Bm", 3), ("c", "A", 3, 1), ("w", "YP2", -3), ("w", "ZL", "Bm", 3), ("c", "A", 2, 0), ("w", "ZR", "B2", 3),
    ("c", "A", 2, 1), ("w", "ZL", "B2", 3), ("w", "ZR", "Bm", 4), ("c", "B", 3, 0), ("c", "B", 3, 1), ("w", "ZR", "B2", 4),
    ("c", "B", 2, 0), ("c", "B", 2, 1),
)
OPENS = {("ZR", "A", 4): ("Bm",), ("YB", "M"): ("Bp",), ("ZL", "B0", 4): ("B2",)}

Z_IDS = [(side, s, i + 1) for s, (r, l) in TURNS.items() for side, n in (("ZR", r), ("ZL", l)) for i in range(n)]
Y_IDS = [(kind, o) for kind in ("YP", "YM") for o in OFFSETS]
Y_IDS += [("YP2", o) for o in UPWARDS] + [("YM2", o) for o in OFFSETS if o not in UPWARDS]
Y_IDS += [("YB", "P"), ("YB", "M"), ("YB", "2")]
G_IDS = Z_IDS + Y_IDS
N_GATHER = len(G_IDS)
NUMBER = {name: i for i, name in enumerate(G_IDS)}


def kernel(
    q_ref, k_ref, v_ref, picks_ref, router_ref, stream_ref, w_hbm, out_ref,
    part_a, part_b, va, row_max, acc, w, att, sib_out, sib_in, hop_out, hop_in, end_out, end_in, total,
    send_sem, recv_sem, sib_send, sib_recv, x_send, x_recv, w_sem,
):
    ctx, ten = lax.axis_index("context"), lax.axis_index("tensor")
    y, z = ctx // NZ, lax.rem(ctx, NZ)
    x, core = ten // 2, lax.rem(ten, 2)

    def wrap(i, n):
        return lax.rem(i + 2 * n, n)

    def at_ctx(yy, zz):
        return (wrap(yy, NY) * NZ + wrap(zz, NZ), ten)

    def at_ten(xx, cc):
        return (ctx, wrap(xx, NX) * 2 + cc)

    up, down, right, left = at_ctx(y + 1, z), at_ctx(y - 1, z), at_ctx(y, z + 1), at_ctx(y, z - 1)
    sibling, x_up, x_down = at_ten(x, 1 - core), at_ten(x + 1, core), at_ten(x - 1, core)

    w_copy = pltpu.make_async_copy(w_hbm, w, w_sem)
    w_copy.start()

    barrier = pltpu.get_barrier_semaphore()
    peers = (up, down, right, left, sibling, x_up, x_down)
    for peer in peers:
        pl.semaphore_signal(barrier, inc=1, device_id=peer, device_id_type=MESH)

    count = jnp.sum(jnp.where(picks_ref[...] < TOK_DEV, 1.0, 0.0), axis=1, keepdims=True)
    row_id = lax.broadcasted_iota(jnp.int32, (CAP, HD), 0)
    valid = row_id.astype(jnp.float32) < count
    k_all, v_all = k_ref[...], v_ref[...]
    k_out = jnp.where(valid, k_all.astype(jnp.float32), k_all[:1].astype(jnp.float32)).astype(jnp.bfloat16)
    v_out = jnp.where(valid, v_all.astype(jnp.float32), FILL).astype(jnp.bfloat16)

    def slot(part, yy, zz):
        rows = ROWS[part]
        start = pl.multiple_of((wrap(yy, NY) * NZ + wrap(zz, NZ)) * rows, 16)
        return (part_a if part == "A" else part_b).at[pl.ds(start, rows), :]

    for part in ("A", "B"):
        rows = slice(FIRST[part], FIRST[part] + ROWS[part])
        own = slot(part, y, z)
        own[:, :HD] = k_out[rows]
        own[:, HD:] = v_out[rows]

    def ends(name):
        kind = name[0]
        if kind in ("ZR", "ZL"):
            _, stream, step = name
            part, yy = stream[0], y + ROW_OF[stream]
            if kind == "ZR":
                return slot(part, yy, z - step + 1), slot(part, yy, z - step), right
            return slot(part, yy, z + step - 1), slot(part, yy, z + step), left
        if kind == "YB":
            if name[1] == "P":
                return slot("B", y, z), slot("B", y - 1, z), up
            if name[1] == "M":
                return slot("B", y, z), slot("B", y + 1, z), down
            return slot("B", y - 1, z), slot("B", y - 2, z), up
        zz = z + name[1]
        if kind == "YP":
            return slot("A", y, zz), slot("A", y - 1, zz), up
        if kind == "YM":
            return slot("A", y, zz), slot("A", y + 1, zz), down
        if kind == "YP2":
            return slot("A", y - 1, zz), slot("A", y - 2, zz), up
        return slot("A", y + 1, zz), slot("A", y + 2, zz), down

    def outgoing(name):
        i = NUMBER[name]
        src, _, target = ends(name)
        return pltpu.make_async_remote_copy(
            src, src, send_sem.at[i], recv_sem.at[i], device_id=target, device_id_type=MESH
        )

    def incoming(name):
        i = NUMBER[name]
        _, dst, target = ends(name)
        return pltpu.make_async_remote_copy(
            dst, dst, send_sem.at[i], recv_sem.at[i], device_id=target, device_id_type=MESH
        )

    def start(name):
        outgoing(name).start()

    def open_ring(stream):
        start(("ZR", stream, 1))
        start(("ZL", stream, 1))

    def arrive(name):
        incoming(name).wait_recv()
        kind = name[0]
        if kind in ("ZR", "ZL"):
            _, stream, step = name
            if step < TURNS[stream][0 if kind == "ZR" else 1]:
                start((kind, stream, step + 1))
            if stream == "A":
                offset = step if kind == "ZL" else (-step if step < 4 else 4)
                start(("YP", offset))
                start(("YM", offset))
        elif kind == "YP" and name[1] in UPWARDS:
            start(("YP2", name[1]))
        elif kind == "YM" and name[1] not in UPWARDS:
            start(("YM2", name[1]))
        elif name == ("YB", "P"):
            start(("YB", "2"))
        for stream in OPENS.get(name, ()):
            open_ring(stream)

    def q_tile(t):
        g, half = t // 2, t % 2
        return q_ref[half * TILE : (half + 1) * TILE, g * HD : (g + 1) * HD]

    def qk(t, keys):
        return lax.dot_general(q_tile(t), keys, (((1,), (1,)), ((), ())), preferred_element_type=jnp.float32)

    def diagonal(half):
        if half == 0:
            va[:CAP, :HD] = v_ref[...]
            va[:CAP, HD:] = jnp.ones((CAP, HD), jnp.bfloat16)
        for t in range(half * 4, half * 4 + 4):
            rows = pl.ds(t * TILE, TILE)
            scores = qk(t, k_ref[...])
            i = lax.broadcasted_iota(jnp.int32, scores.shape, 0) + (t % 2) * TILE
            j = lax.broadcasted_iota(jnp.int32, scores.shape, 1)
            scores = jnp.where(j <= i, scores, NEG)
            top = jnp.max(scores, axis=1, keepdims=True)
            weights = jnp.exp2((scores - top) * KAPPA).astype(jnp.bfloat16)
            acc[rows, :] = jnp.dot(weights, va[:CAP, :], preferred_element_type=jnp.float32)
            row_max[rows, :] = jnp.broadcast_to(top, (TILE, HD))

    def unit(part, rho, half):
        n = NZ * ROWS[part]
        yy = wrap(y + rho, NY)
        first = pl.multiple_of(yy * n, n)
        ref = part_a if part == "A" else part_b

        @pl.when(z > 0 if rho == 0 else yy < y)
        def _():
            if half == 0:
                block = ref[pl.ds(first, n), HD:]
                real = block < FILL / 2
                va[:n, :HD] = jnp.where(real, block, 0).astype(jnp.bfloat16)
                va[:n, HD:] = jnp.where(real, 1, 0).astype(jnp.bfloat16)
            for t in range(half * 4, half * 4 + 4):
                rows = pl.ds(t * TILE, TILE)
                scores = qk(t, ref[pl.ds(first, n), :HD])
                if rho == 0:
                    j = lax.broadcasted_iota(jnp.int32, scores.shape, 1)
                    scores = jnp.where(j < z * ROWS[part], scores, NEG)
                old = row_max[rows, :]
                new = jnp.maximum(old, jnp.max(scores, axis=1, keepdims=True))
                weights = jnp.exp2((scores - new[:, :1]) * KAPPA).astype(jnp.bfloat16)
                factor = jnp.exp2((old - new) * KAPPA)
                more = jnp.dot(weights, va[:n, :], preferred_element_type=jnp.float32)
                acc[rows, :HD] = acc[rows, :HD] * factor + more[:, :HD]
                acc[rows, HD:] = acc[rows, HD:] * factor + more[:, HD:]
                row_max[rows, :] = new

    pl.semaphore_wait(barrier, len(peers))
    start(("YB", "P"))
    start(("YB", "M"))
    open_ring("A")
    start(("YP", 0))
    start(("YM", 0))
    open_ring("B0")

    for what, *rest in ORDER:
        if what == "w":
            arrive(tuple(rest))
        elif rest[0] == "diag":
            diagonal(rest[1])
        else:
            unit(*rest)

    for t in range(8):
        g, half = t // 2, t % 2
        rows = pl.ds(t * TILE, TILE)
        att[half * TILE : (half + 1) * TILE, g * HD : (g + 1) * HD] = (acc[rows, :HD] / acc[rows, HD:]).astype(jnp.bfloat16)

    w_copy.wait()

    def partial(d, cc):
        cols = pl.ds(pl.multiple_of((wrap(x + d, NX) * 2 + cc) * WIDTH, 128), WIDTH)
        return jnp.dot(att[...], w[:, cols], preferred_element_type=jnp.float32)

    def to_sibling(d):
        return pltpu.make_async_remote_copy(
            sib_out.at[d], sib_in.at[d], sib_send.at[d], sib_recv.at[d], device_id=sibling, device_id_type=MESH
        )

    lo, hi = pl.ds(0, TILE), pl.ds(TILE, TILE)

    def x_copy(i, src, dst, target):
        return pltpu.make_async_remote_copy(
            src, dst, x_send.at[i], x_recv.at[i], device_id=target, device_id_type=MESH
        )

    hop_up = x_copy(0, hop_out.at[lo], hop_in.at[lo], x_up)
    hop_down = x_copy(1, hop_out.at[hi], hop_in.at[hi], x_down)
    up_hi = x_copy(2, end_out.at[0, hi], end_in.at[0, hi], x_up)
    up_lo = x_copy(3, end_out.at[0, lo], end_in.at[0, lo], x_up)
    down_lo = x_copy(4, end_out.at[1, lo], end_in.at[1, lo], x_down)
    down_hi = x_copy(5, end_out.at[1, hi], end_in.at[1, hi], x_down)

    def send_sibling(d):
        sib_out[d] = partial(d, 1 - core).astype(jnp.bfloat16)
        to_sibling(d).start()

    def chip_sum(d):
        own = partial(d, core)
        to_sibling(d).wait_recv()
        return own + sib_in[d].astype(jnp.float32)

    send_sibling(2)
    send_sibling(1)
    hop_out[...] = chip_sum(2).astype(jnp.bfloat16)
    hop_up.start()
    hop_down.start()
    send_sibling(3)
    total[...] = chip_sum(1)
    end_out[0, hi] = total[hi, :].astype(jnp.bfloat16)
    up_hi.start()
    hop_up.wait_recv()
    end_out[0, lo] = (total[lo, :] + hop_in[lo, :].astype(jnp.float32)).astype(jnp.bfloat16)
    up_lo.start()
    total[...] = chip_sum(3)
    end_out[1, lo] = total[lo, :].astype(jnp.bfloat16)
    down_lo.start()
    hop_down.wait_recv()
    end_out[1, hi] = (total[hi, :] + hop_in[hi, :].astype(jnp.float32)).astype(jnp.bfloat16)
    down_hi.start()
    send_sibling(0)
    total[...] = chip_sum(0)

    router = router_ref[...]
    eye = lax.broadcasted_iota(jnp.int32, (CAP, CAP), 0) == lax.broadcasted_iota(jnp.int32, (CAP, CAP), 1)
    gain = jnp.sum(jnp.where(eye, router, 0.0), axis=1, keepdims=True)
    wide_valid = lax.broadcasted_iota(jnp.int32, (CAP, WIDTH), 0).astype(jnp.float32) < count

    def finish(rows, first, second):
        first.wait_recv()
        second.wait_recv()
        here = slice(0, TILE) if rows is lo else slice(TILE, CAP)
        projected = total[rows, :] + end_in[0, rows].astype(jnp.float32) + end_in[1, rows].astype(jnp.float32)
        residual = stream_ref[rows, :].astype(jnp.float32)
        updated = jnp.where(wide_valid[here], residual + gain[here] * projected, residual)
        out_ref[rows, :] = updated.astype(jnp.bfloat16)

    finish(lo, down_lo, up_lo)
    finish(hi, up_hi, down_hi)

    for name in G_IDS:
        outgoing(name).wait_send()
    for d in range(NX):
        to_sibling(d).wait_send()
    for copy in (hop_up, hop_down, up_hi, up_lo, down_lo, down_hi):
        copy.wait_send()


def local(stream_rows, picks, router, queries, keys, values, out_weight):
    vmem = pl.BlockSpec(memory_space=pltpu.VMEM)
    bf16, f32 = jnp.bfloat16, jnp.float32
    dma = pltpu.SemaphoreType.DMA
    return pl.pallas_call(
        kernel,
        out_shape=jax.ShapeDtypeStruct(stream_rows.shape, bf16),
        in_specs=[vmem] * 6 + [pl.BlockSpec(memory_space=pl.ANY)],
        out_specs=vmem,
        scratch_shapes=[
            pltpu.VMEM((NY * NZ * ROWS["A"], 2 * HD), bf16),
            pltpu.VMEM((NY * NZ * ROWS["B"], 2 * HD), bf16),
            pltpu.VMEM((NZ * ROWS["A"], 2 * HD), bf16),
            pltpu.VMEM((GROUP * CAP, HD), f32),
            pltpu.VMEM((GROUP * CAP, 2 * HD), f32),
            pltpu.VMEM(out_weight.shape, bf16),
            pltpu.VMEM((CAP, GROUP * HD), bf16),
            pltpu.VMEM((NX, CAP, WIDTH), bf16),
            pltpu.VMEM((NX, CAP, WIDTH), bf16),
            pltpu.VMEM((CAP, WIDTH), bf16),
            pltpu.VMEM((CAP, WIDTH), bf16),
            pltpu.VMEM((2, CAP, WIDTH), bf16),
            pltpu.VMEM((2, CAP, WIDTH), bf16),
            pltpu.VMEM((CAP, WIDTH), f32),
            dma((N_GATHER,)),
            dma((N_GATHER,)),
            dma((NX,)),
            dma((NX,)),
            dma((6,)),
            dma((6,)),
            dma,
        ],
        compiler_params=pltpu.CompilerParams(
            collective_id=0, has_side_effects=True, vmem_limit_bytes=56 * 2**20
        ),
        cost_estimate=pl.CostEstimate(flops=8 * 10**9, bytes_accessed=10**7, transcendentals=10**7),
    )(queries, keys, values, picks.reshape(1, CAP), router.reshape(1, CAP), stream_rows, out_weight)


def solution(mesh):
    placed = (
        P("context", "tensor"),
        P("context"),
        P("context"),
        P("context", "tensor"),
        P("context", "tensor"),
        P("context", "tensor"),
        P("tensor", None),
    )
    return jax.shard_map(
        local, mesh=mesh, in_specs=placed, out_specs=P("context", "tensor"), check_vma=False
    )
```

```python
import jax
import jax.numpy as jnp
from jax import lax
from jax.experimental import pallas as pl
from jax.experimental.pallas import tpu as pltpu
from jax.sharding import PartitionSpec as P

MESH = pl.DeviceIdType.MESH

TOK_DEV = 1536
CAP = 288
HD = 128
NY, NZ, NX = 4, 8, 4
WIDTH = 896
GROUP = 4
KAPPA = 128**-0.5 * 1.4426950408889634
NEG = -1e30
FILL = 64.0
TILE = 144

ROWS = {"A": 176, "B": 112}
FIRST = {"A": 0, "B": 176}
TURNS = {"A": (4, 3), "B0": (4, 3), "Bm": (3, 4), "Bp": (3, 4), "B2": (3, 4)}
ROW_OF = {"A": 0, "B0": 0, "Bm": 3, "Bp": 1, "B2": 2}
OFFSETS = (0, -1, -2, -3, 4, 1, 2, 3)
UPWARDS = (0, -1, -2, -3)
FIRST_SENDS = ("YB", "A", "YA", "B0")
UNITS = (
    (("YB", "P"), ("YB", "M"), ("ZR", "A", 1), ("ZL", "A", 1),),
    (("YP", 0), ("YM", 0), ("ZR", "B0", 1), ("ZL", "B0", 1),),
    (("YB", "2"), ("ZR", "A", 2), ("YM", -1), ("ZL", "A", 2),),
    (("YP", -1), ("ZR", "B0", 2), ("ZL", "B0", 2), ("YM", 1),),
    (("YP", 1), ("ZR", "Bp", 1), ("ZL", "Bp", 1), ("ZL", "B2", 1),),
    (("YM", -2), ("YP2", 0), ("ZR", "A", 3),),
    (("ZR", "B2", 1), ("ZL", "A", 3), ("YM", 2), ("YP", -2), ("ZR", "Bm", 1),),
    (("ZL", "Bm", 1), ("YM2", 1), ("ZR", "B0", 3), ("ZL", "B0", 3),),
    (("YP", 2), ("ZR", "Bp", 2), ("ZL", "Bp", 2), ("YM", -3), ("YP2", -1),),
    (("ZL", "B2", 2), ("ZR", "A", 4), ("ZL", "Bm", 2), ("YM", 3), ("YP", -3),),
    (("ZR", "B2", 2), ("ZL", "Bp", 3), ("ZR", "Bm", 2), ("YM2", 2),),
    (("YP", 3), ("ZL", "B2", 3), ("ZR", "B0", 4), ("YM", 4), ("ZL", "Bm", 3), ("YP2", -2), ("ZR", "Bp", 3),),
    (("ZL", "Bp", 4), ("ZR", "B2", 3), ("YM2", 3), ("YP", 4), ("ZL", "B2", 4),),
    (("ZR", "Bm", 3), ("ZL", "Bm", 4), ("YP2", -3), ("YM2", 4),),
)
ORDER = (
    ("c", "diag", 0), ("c", "diag", 1), ("w", "YB", "P"), ("w", "YB", "M"), ("w", "ZR", "A", 1), ("w", "ZL", "A", 1),
    ("c", 0, 0), ("c", 0, 1), ("w", "YP", 0), ("w", "YM", 0), ("w", "ZR", "B0", 1), ("w", "ZL", "B0", 1),
    ("c", 1, 0), ("c", 1, 1), ("w", "YB", "2"), ("w", "ZR", "A", 2), ("w", "YM", -1), ("w", "ZL", "A", 2),
    ("c", 2, 0), ("w", "YP", -1), ("c", 2, 1), ("w", "ZR", "B0", 2), ("w", "ZL", "B0", 2), ("w", "YM", 1),
    ("c", 3, 0), ("w", "YP", 1), ("w", "ZR", "Bp", 1), ("w", "ZL", "Bp", 1), ("c", 3, 1), ("w", "ZL", "B2", 1),
    ("c", 4, 0), ("w", "YM", -2), ("w", "YP2", 0), ("w", "ZR", "A", 3), ("c", 4, 1), ("c", 5, 0),
    ("w", "ZR", "B2", 1), ("w", "ZL", "A", 3), ("w", "YM", 2), ("c", 5, 1), ("w", "YP", -2), ("w", "ZR", "Bm", 1),
    ("w", "ZL", "Bm", 1), ("c", 6, 0), ("w", "YM2", 1), ("w", "ZR", "B0", 3), ("w", "ZL", "B0", 3), ("w", "YP", 2),
    ("c", 6, 1), ("c", 7, 0), ("w", "ZR", "Bp", 2), ("w", "ZL", "Bp", 2), ("c", 7, 1), ("w", "YM", -3),
    ("w", "YP2", -1), ("w", "ZL", "B2", 2), ("c", 8, 0), ("w", "ZR", "A", 4), ("c", 8, 1), ("w", "ZL", "Bm", 2),
    ("w", "YM", 3), ("w", "YP", -3), ("w", "ZR", "B2", 2), ("c", 9, 0), ("w", "ZL", "Bp", 3), ("c", 9, 1),
    ("w", "ZR", "Bm", 2), ("w", "YM2", 2), ("w", "YP", 3), ("w", "ZL", "B2", 3), ("c", 10, 0), ("w", "ZR", "B0", 4),
    ("c", 10, 1), ("w", "YM", 4), ("w", "ZL", "Bm", 3), ("w", "YP2", -2), ("w", "ZR", "Bp", 3), ("c", 11, 0),
    ("w", "ZL", "Bp", 4), ("w", "ZR", "B2", 3), ("c", 11, 1), ("w", "YM2", 3), ("w", "YP", 4), ("w", "ZL", "B2", 4),
    ("w", "ZR", "Bm", 3), ("c", 12, 0), ("w", "ZL", "Bm", 4), ("c", 12, 1), ("w", "YP2", -3), ("w", "YM2", 4),
    ("c", 13, 0), ("c", 13, 1),
)
OPENS = {
    ("ZL", "B0", 1): ("Bp",),
    ("ZR", "A", 2): ("B2",),
    ("ZL", "A", 2): ("Bm",),
}

Z_IDS = [(side, s, i + 1) for s, (r, l) in TURNS.items() for side, n in (("ZR", r), ("ZL", l)) for i in range(n)]
Y_IDS = [(kind, o) for kind in ("YP", "YM") for o in OFFSETS]
Y_IDS += [("YP2", o) for o in UPWARDS] + [("YM2", o) for o in OFFSETS if o not in UPWARDS]
Y_IDS += [("YB", "P"), ("YB", "M"), ("YB", "2")]
G_IDS = Z_IDS + Y_IDS
N_GATHER = len(G_IDS)
NUMBER = {name: i for i, name in enumerate(G_IDS)}


def part_of(name):
    return "A" if name[1] == "A" or (name[0][0] == "Y" and name[0] != "YB") else "B"


PLACE, UNIT_ROWS = {}, []
for unit_pieces in UNITS:
    begin = sum(UNIT_ROWS)
    end = begin
    for piece in unit_pieces:
        PLACE[piece] = end
        end += ROWS[part_of(piece)]
    UNIT_ROWS.append(end - begin)

BLOCKS = (((0, 80), (80, 64)), ((144, 64), (208, 80)))


def kernel(
    q_ref, k_ref, v_ref, picks_ref, router_ref, stream_ref, w_hbm, out_ref,
    own, held, va, row_max, acc, w, att, sib_out, sib_in, hop_out, hop_in, end_out, end_in, total,
    send_sem, recv_sem, sib_send, sib_recv, x_send, x_recv, w_sem,
):
    ctx, ten = lax.axis_index("context"), lax.axis_index("tensor")
    y, z = ctx // NZ, lax.rem(ctx, NZ)
    x, core = ten // 2, lax.rem(ten, 2)

    def wrap(i, n):
        return lax.rem(i + 2 * n, n)

    def at_ctx(yy, zz):
        return (wrap(yy, NY) * NZ + wrap(zz, NZ), ten)

    def at_ten(xx, cc):
        return (ctx, wrap(xx, NX) * 2 + cc)

    up, down, right, left = at_ctx(y + 1, z), at_ctx(y - 1, z), at_ctx(y, z + 1), at_ctx(y, z - 1)
    sibling, x_up, x_down = at_ten(x, 1 - core), at_ten(x + 1, core), at_ten(x - 1, core)

    barrier = pltpu.get_barrier_semaphore()
    peers = (up, down, right, left, sibling, x_up, x_down)
    for peer in peers:
        pl.semaphore_signal(barrier, inc=1, device_id=peer, device_id_type=MESH)

    w_copy = pltpu.make_async_copy(w_hbm, w, w_sem)
    w_copy.start()

    picks = picks_ref[...].reshape(1, CAP)
    count = jnp.sum(jnp.where(picks < TOK_DEV, 1.0, 0.0), axis=1, keepdims=True)
    row_id = lax.broadcasted_iota(jnp.int32, (CAP, HD), 0)
    valid = row_id.astype(jnp.float32) < count
    k_all, v_all = k_ref[...], v_ref[...]
    own[:, :HD] = jnp.where(valid, k_all.astype(jnp.float32), k_all[:1].astype(jnp.float32)).astype(jnp.bfloat16)
    own[:, HD:] = jnp.where(valid, v_all.astype(jnp.float32), FILL).astype(jnp.bfloat16)

    def place(name):
        return held.at[pl.ds(PLACE[name], ROWS[part_of(name)]), :]

    def own_part(part):
        return own.at[pl.ds(FIRST[part], ROWS[part]), :]

    def own_row(offset):
        if offset == 0:
            return own_part("A")
        name = ("ZL", "A", offset) if 0 < offset < 4 else ("ZR", "A", -offset if offset < 0 else 4)
        return place(name)

    def source(name):
        kind = name[0]
        if kind in ("ZR", "ZL"):
            _, stream, step = name
            target = right if kind == "ZR" else left
            if step > 1:
                return place((kind, stream, step - 1)), target
            if stream in ("A", "B0"):
                return own_part(stream[0]), target
            return place(("YB", {"Bm": "P", "Bp": "M", "B2": "2"}[stream])), target
        if kind == "YB":
            return (place(("YB", "P")) if name[1] == "2" else own_part("B")), (down if name[1] == "M" else up)
        if kind == "YP":
            return own_row(name[1]), up
        if kind == "YM":
            return own_row(name[1]), down
        if kind == "YP2":
            return place(("YP", name[1])), up
        return place(("YM", name[1])), down

    def shard(name):
        kind = name[0]
        if kind in ("ZR", "ZL"):
            return wrap(y + ROW_OF[name[1]], NY), wrap(z - name[2] if kind == "ZR" else z + name[2], NZ)
        if kind == "YB":
            return wrap(y + {"P": -1, "M": 1, "2": 2}[name[1]], NY), z
        return wrap(y + {"YP": -1, "YM": 1, "YP2": 2, "YM2": 2}[kind], NY), wrap(z + name[1], NZ)

    def transfer(name):
        i = NUMBER[name]
        src, target = source(name)
        return pltpu.make_async_remote_copy(
            src, place(name), send_sem.at[i], recv_sem.at[i], device_id=target, device_id_type=MESH
        )

    def start(name):
        transfer(name).start()

    def open_ring(stream):
        start(("ZR", stream, 1))
        start(("ZL", stream, 1))

    def open_column(offset):
        start(("YP", offset))
        start(("YM", offset))

    def arrive(name):
        transfer(name).wait_recv()
        kind = name[0]
        if kind in ("ZR", "ZL"):
            _, stream, step = name
            if step < TURNS[stream][0 if kind == "ZR" else 1]:
                start((kind, stream, step + 1))
            if stream == "A":
                open_column(step if kind == "ZL" else (-step if step < 4 else 4))
        elif kind == "YP" and name[1] in UPWARDS:
            start(("YP2", name[1]))
        elif kind == "YM" and name[1] not in UPWARDS:
            start(("YM2", name[1]))
        elif name == ("YB", "P"):
            start(("YB", "2"))
        for stream in OPENS.get(name, ()):
            open_ring(stream)

    def qk(g, half, keys):
        q = q_ref[half * TILE : (half + 1) * TILE, g * HD : (g + 1) * HD]
        return lax.dot_general(q, keys, (((1,), (1,)), ((), ())), preferred_element_type=jnp.float32)

    def tile(g, half):
        return pl.ds((half * GROUP + g) * TILE, TILE)

    def diagonal(half):
        if half == 0:
            va[:CAP, :HD] = v_ref[...]
            va[:CAP, HD:] = jnp.ones((CAP, HD), jnp.bfloat16)
        for g in range(GROUP):
            rows = tile(g, half)
            scores = qk(g, half, k_ref[...])
            i = lax.broadcasted_iota(jnp.int32, scores.shape, 0) + half * TILE
            j = lax.broadcasted_iota(jnp.int32, scores.shape, 1)
            scores = jnp.where(j <= i, scores, NEG)
            top = jnp.max(scores, axis=1, keepdims=True)
            weights = jnp.exp2((scores - top) * KAPPA).astype(jnp.bfloat16)
            acc[rows, :] = jnp.dot(weights, va[:CAP, :], preferred_element_type=jnp.float32)
            row_max[rows, :] = jnp.broadcast_to(top, (TILE, HD))

    def unit(u, half):
        n = UNIT_ROWS[u]
        here = pl.ds(PLACE[UNITS[u][0]], n)
        seen = []
        for name in UNITS[u]:
            yy, zz = shard(name)
            seen.append(jnp.logical_or(yy < y, jnp.logical_and(yy == y, zz < z)))
        some = seen[0]
        for other in seen[1:]:
            some = jnp.logical_or(some, other)

        @pl.when(some)
        def _():
            if half == 0:
                block = held[here, HD:]
                real = block < FILL / 2
                va[:n, :HD] = jnp.where(real, block, 0).astype(jnp.bfloat16)
                va[:n, HD:] = jnp.where(real, 1, 0).astype(jnp.bfloat16)
            column = lax.broadcasted_iota(jnp.int32, (1, n), 1)
            hide = jnp.zeros((1, n), jnp.float32)
            for name, shown in zip(UNITS[u], seen):
                first = PLACE[name] - PLACE[UNITS[u][0]]
                inside = jnp.logical_and(column >= first, column < first + ROWS[part_of(name)])
                hide = jnp.where(inside, jnp.where(shown, 0.0, NEG), hide)
            for g in range(GROUP):
                rows = tile(g, half)
                scores = qk(g, half, held[here, :HD]) + hide
                old = row_max[rows, :]
                new = jnp.maximum(old, jnp.max(scores, axis=1, keepdims=True))
                weights = jnp.exp2((scores - new[:, :1]) * KAPPA).astype(jnp.bfloat16)
                factor = jnp.exp2((old - new) * KAPPA)
                more = jnp.dot(weights, va[:n, :], preferred_element_type=jnp.float32)
                acc[rows, :HD] = acc[rows, :HD] * factor + more[:, :HD]
                acc[rows, HD:] = acc[rows, HD:] * factor + more[:, HD:]
                row_max[rows, :] = new

    def normalize(half):
        for g in range(GROUP):
            rows = tile(g, half)
            att[half * TILE : (half + 1) * TILE, g * HD : (g + 1) * HD] = (
                acc[rows, :HD] / acc[rows, HD:]
            ).astype(jnp.bfloat16)

    def block_rows(b):
        return pl.ds(b * TILE, TILE)

    def partial(d, cc, b):
        cols = pl.ds(pl.multiple_of((wrap(x + d, NX) * 2 + cc) * WIDTH, 128), WIDTH)
        return jnp.dot(att[block_rows(b), :], w[:, cols], preferred_element_type=jnp.float32)

    def to_sibling(d, b):
        i = 2 * d + b
        return pltpu.make_async_remote_copy(
            sib_out.at[d, block_rows(b)], sib_in.at[d, block_rows(b)], sib_send.at[i], sib_recv.at[i],
            device_id=sibling, device_id_type=MESH,
        )

    def x_copy(kind, way, b):
        i = (kind * 2 + way) * 2 + b
        first, count_rows = BLOCKS[b][way if kind < 2 else 1 - way]
        rows = pl.ds(first, count_rows)
        if kind == 0:
            src, dst = hop_out.at[rows], hop_in.at[rows]
        else:
            src, dst = end_out.at[way, rows], end_in.at[way, rows]
        return pltpu.make_async_remote_copy(
            src, dst, x_send.at[i], x_recv.at[i], device_id=(x_up, x_down)[way], device_id_type=MESH
        )

    def send_sibling(d, b):
        sib_out[d, block_rows(b)] = partial(d, 1 - core, b).astype(jnp.bfloat16)
        to_sibling(d, b).start()

    def chip_sum(d, b):
        mine = partial(d, core, b)
        to_sibling(d, b).wait_recv()
        return mine + sib_in[d, block_rows(b)].astype(jnp.float32)

    def far(b):
        send_sibling(2, b)
        send_sibling(1, b)
        hop_out[block_rows(b), :] = chip_sum(2, b).astype(jnp.bfloat16)
        x_copy(0, 0, b).start()
        x_copy(0, 1, b).start()
        send_sibling(3, b)

    def near(b):
        for way, d in ((0, 1), (1, 3)):
            total[way, block_rows(b)] = chip_sum(d, b)
            first, count_rows = BLOCKS[b][1 - way]
            rows = pl.ds(first, count_rows)
            end_out[way, rows] = total[way, rows].astype(jnp.bfloat16)
            x_copy(2, way, b).start()
        send_sibling(0, b)

    def pass_on(b):
        for way in (0, 1):
            first, count_rows = BLOCKS[b][way]
            rows = pl.ds(first, count_rows)
            x_copy(0, way, b).wait_recv()
            end_out[way, rows] = (total[way, rows] + hop_in[rows, :].astype(jnp.float32)).astype(jnp.bfloat16)
            x_copy(1, way, b).start()

    def finish(b):
        rows = block_rows(b)
        total[0, rows] = chip_sum(0, b)
        for way in (0, 1):
            here = pl.ds(*BLOCKS[b][way])
            x_copy(2, 1 - way, b).wait_recv()
            x_copy(1, way, b).wait_recv()
            projected = total[0, here] + end_in[0, here].astype(jnp.float32) + end_in[1, here].astype(jnp.float32)
            residual = stream_ref[here, :].astype(jnp.float32)
            inside = slice(BLOCKS[b][way][0], sum(BLOCKS[b][way]))
            updated = jnp.where(wide_valid[inside], residual + gain[inside] * projected, residual)
            out_ref[here, :] = updated.astype(jnp.bfloat16)

    pl.semaphore_wait(barrier, len(peers))
    for what in FIRST_SENDS:
        if what == "YB":
            start(("YB", "P"))
            start(("YB", "M"))
        elif what == "YA":
            open_column(0)
        else:
            open_ring(what)

    for what, *rest in ORDER[:-1]:
        if what == "w":
            arrive(tuple(rest))
        elif rest[0] == "diag":
            diagonal(rest[1])
        else:
            unit(*rest)

    normalize(0)
    w_copy.wait()
    far(0)
    unit(*ORDER[-1][1:])
    normalize(1)
    near(0)
    far(1)
    pass_on(0)
    near(1)
    pass_on(1)

    router = router_ref[...].reshape(1, CAP)
    eye = lax.broadcasted_iota(jnp.int32, (CAP, CAP), 0) == lax.broadcasted_iota(jnp.int32, (CAP, CAP), 1)
    gain = jnp.sum(jnp.where(eye, router, 0.0), axis=1, keepdims=True)
    wide_valid = lax.broadcasted_iota(jnp.int32, (CAP, WIDTH), 0).astype(jnp.float32) < count
    finish(0)
    finish(1)

    for name in G_IDS:
        transfer(name).wait_send()
    for b in (0, 1):
        for d in range(NX):
            to_sibling(d, b).wait_send()
        for kind in range(3):
            for way in (0, 1):
                x_copy(kind, way, b).wait_send()


def local(stream_rows, picks, router, queries, keys, values, out_weight):
    vmem = pl.BlockSpec(memory_space=pltpu.VMEM)
    bf16, f32 = jnp.bfloat16, jnp.float32
    dma = pltpu.SemaphoreType.DMA
    return pl.pallas_call(
        kernel,
        out_shape=jax.ShapeDtypeStruct(stream_rows.shape, bf16),
        in_specs=[vmem] * 6 + [pl.BlockSpec(memory_space=pl.ANY)],
        out_specs=vmem,
        scratch_shapes=[
            pltpu.VMEM((CAP, 2 * HD), bf16),
            pltpu.VMEM((sum(UNIT_ROWS), 2 * HD), bf16),
            pltpu.VMEM((max(UNIT_ROWS), 2 * HD), bf16),
            pltpu.VMEM((GROUP * CAP, HD), f32),
            pltpu.VMEM((GROUP * CAP, 2 * HD), f32),
            pltpu.VMEM(out_weight.shape, bf16),
            pltpu.VMEM((CAP, GROUP * HD), bf16),
            pltpu.VMEM((NX, CAP, WIDTH), bf16),
            pltpu.VMEM((NX, CAP, WIDTH), bf16),
            pltpu.VMEM((CAP, WIDTH), bf16),
            pltpu.VMEM((CAP, WIDTH), bf16),
            pltpu.VMEM((2, CAP, WIDTH), bf16),
            pltpu.VMEM((2, CAP, WIDTH), bf16),
            pltpu.VMEM((2, CAP, WIDTH), f32),
            dma((N_GATHER,)),
            dma((N_GATHER,)),
            dma((2 * NX,)),
            dma((2 * NX,)),
            dma((12,)),
            dma((12,)),
            dma,
        ],
        compiler_params=pltpu.CompilerParams(
            collective_id=0, has_side_effects=True, vmem_limit_bytes=56 * 2**20
        ),
        cost_estimate=pl.CostEstimate(flops=8 * 10**9, bytes_accessed=10**7, transcendentals=10**7),
    )(queries, keys, values, picks, router, stream_rows, out_weight)


def solution(mesh):
    placed = (
        P("context", "tensor"),
        P("context"),
        P("context"),
        P("context", "tensor"),
        P("context", "tensor"),
        P("context", "tensor"),
        P("tensor", None),
    )
    return jax.shard_map(
        local, mesh=mesh, in_specs=placed, out_specs=P("context", "tensor"), check_vma=False
    )
```

```python
import jax
import jax.numpy as jnp
from jax import lax
from jax.experimental import pallas as pl
from jax.experimental.pallas import tpu as pltpu
from jax.sharding import PartitionSpec as P

MESH = pl.DeviceIdType.MESH

TOK_DEV = 1536
CAP = 288
HD = 128
NY, NZ, NX = 4, 8, 4
WIDTH = 896
GROUP = 4
KAPPA = 128**-0.5 * 1.4426950408889634
NEG = -1e30
FILL = 64.0
TILE = 144

ROWS = {"A": 192, "B": 96}
FIRST = {"A": 0, "B": 192}
TURNS = {"A": (4, 3), "B0": (3, 4), "Bm": (3, 4), "Bp": (3, 4), "B2": (4, 3)}
ROW_OF = {"A": 0, "B0": 0, "Bm": 3, "Bp": 1, "B2": 2}
OFFSETS = (0, -1, -2, -3, 4, 1, 2, 3)
UPWARDS = (0, -1, -2, -3)
FIRST_SENDS = ("YB", "A", "YA", "B0")
UNITS = (
    (("ZR", "A", 1), ("ZL", "A", 1), ("YB", "P"), ("YB", "M"), ("ZR", "B0", 1), ("ZL", "B0", 1),),
    (("YP", 0), ("YM", 0), ("ZR", "A", 2), ("YB", "2"), ("ZR", "Bm", 1),),
    (("YP", -1), ("YM", -1), ("ZL", "Bm", 1), ("ZR", "B0", 2), ("ZL", "B0", 2), ("ZR", "Bm", 2),),
    (("ZL", "A", 2), ("YP", 1), ("YM", 1), ("YP2", 0),),
    (("ZR", "A", 3), ("YM", -2), ("ZL", "Bm", 2), ("ZR", "B0", 3), ("ZL", "Bp", 1), ("ZR", "Bp", 1),),
    (("ZL", "A", 3), ("YP", -2), ("ZL", "B0", 3), ("ZR", "Bm", 3), ("ZL", "Bm", 3), ("ZR", "B2", 1),),
    (("YM", 2), ("YP2", -1), ("YM2", 1), ("ZL", "B2", 1), ("ZL", "Bp", 2),),
    (("YP", 2), ("YM", -3), ("ZL", "B0", 4), ("ZR", "Bp", 2), ("ZL", "Bm", 4), ("ZR", "B2", 2),),
    (("ZR", "A", 4), ("YP", -3), ("YM", 3), ("ZL", "B2", 2), ("ZL", "Bp", 3),),
    (("YP", 3), ("YM2", 2), ("YP2", -2), ("ZR", "Bp", 3), ("ZR", "B2", 3),),
    (("YM", 4), ("YP", 4), ("YM2", 3), ("ZL", "B2", 3), ("ZL", "Bp", 4),),
    (("YP2", -3), ("YM2", 4), ("ZR", "B2", 4),),
)
ORDER = (
    ("c", "diag"), ("w", "YB", "P"), ("w", "YB", "M"), ("w", "ZR", "A", 1), ("w", "ZL", "A", 1),
    ("w", "YP", 0), ("w", "YM", 0), ("w", "ZR", "B0", 1), ("w", "ZL", "B0", 1), ("c", 0), ("w", "YB", "2"),
    ("w", "ZR", "Bm", 1), ("w", "ZL", "Bm", 1), ("w", "ZR", "A", 2), ("w", "YP", -1), ("w", "YM", -1),
    ("w", "ZL", "A", 2), ("c", 1), ("w", "ZR", "B0", 2), ("w", "ZL", "B0", 2), ("w", "YP", 1), ("w", "YM", 1),
    ("w", "ZR", "Bm", 2), ("w", "ZL", "Bm", 2), ("c", 2), ("w", "YP2", 0), ("c", 3), ("w", "ZR", "A", 3),
    ("w", "YM", -2), ("w", "ZL", "A", 3), ("w", "ZR", "B0", 3), ("w", "ZL", "Bp", 1), ("w", "YP", -2),
    ("w", "YM", 2), ("w", "ZR", "Bp", 1), ("c", 4), ("w", "ZL", "B0", 3), ("w", "ZR", "Bm", 3),
    ("w", "ZL", "Bm", 3), ("w", "YP2", -1), ("w", "YM2", 1), ("w", "ZR", "B2", 1), ("w", "ZL", "B2", 1), ("c", 5),
    ("w", "ZL", "Bp", 2), ("w", "YP", 2), ("w", "YM", -3), ("w", "ZR", "A", 4), ("c", 6), ("w", "ZL", "B0", 4),
    ("w", "ZR", "Bp", 2), ("w", "YP", -3), ("w", "ZL", "Bm", 4), ("w", "YM", 3), ("w", "ZR", "B2", 2), ("c", 7),
    ("w", "ZL", "B2", 2), ("w", "YP", 3), ("w", "ZL", "Bp", 3), ("w", "YM2", 2), ("c", 8), ("w", "ZR", "Bp", 3),
    ("w", "YP2", -2), ("w", "YM", 4), ("w", "ZR", "B2", 3), ("c", 9), ("w", "ZL", "B2", 3), ("w", "YP", 4),
    ("w", "YM2", 3), ("w", "ZL", "Bp", 4), ("c", 10), ("w", "ZR", "B2", 4), ("w", "YP2", -3), ("w", "YM2", 4),
    ("c", 11),
)
OPENS = {
    ("YB", "P"): ("Bm",),
    ("ZR", "B0", 2): ("Bp",),
    ("ZL", "Bm", 2): ("B2",),
}

Z_IDS = [(side, s, i + 1) for s, (r, l) in TURNS.items() for side, n in (("ZR", r), ("ZL", l)) for i in range(n)]
Y_IDS = [(kind, o) for kind in ("YP", "YM") for o in OFFSETS]
Y_IDS += [("YP2", o) for o in UPWARDS] + [("YM2", o) for o in OFFSETS if o not in UPWARDS]
Y_IDS += [("YB", "P"), ("YB", "M"), ("YB", "2")]
G_IDS = Z_IDS + Y_IDS
N_GATHER = len(G_IDS)
NUMBER = {name: i for i, name in enumerate(G_IDS)}


def part_of(name):
    return "A" if name[1] == "A" or (name[0][0] == "Y" and name[0] != "YB") else "B"


PLACE, UNIT_ROWS = {}, []
for unit_pieces in UNITS:
    begin = sum(UNIT_ROWS)
    end = begin
    for piece in unit_pieces:
        PLACE[piece] = end
        end += ROWS[part_of(piece)]
    UNIT_ROWS.append(end - begin)

BLOCKS = (((0, 80), (80, 64)), ((144, 64), (208, 80)))


def kernel(
    q_ref, k_ref, v_ref, picks_ref, router_ref, stream_ref, w_hbm, out_ref,
    own, held, va, row_max, acc, w, att, sib_out, sib_in, hop_out, hop_in, end_out, end_in, total,
    send_sem, recv_sem, sib_send, sib_recv, x_send, x_recv, w_sem,
):
    ctx, ten = lax.axis_index("context"), lax.axis_index("tensor")
    y, z = ctx // NZ, lax.rem(ctx, NZ)
    x, core = ten // 2, lax.rem(ten, 2)

    def wrap(i, n):
        return lax.rem(i + 2 * n, n)

    def at_ctx(yy, zz):
        return (wrap(yy, NY) * NZ + wrap(zz, NZ), ten)

    def at_ten(xx, cc):
        return (ctx, wrap(xx, NX) * 2 + cc)

    up, down, right, left = at_ctx(y + 1, z), at_ctx(y - 1, z), at_ctx(y, z + 1), at_ctx(y, z - 1)
    sibling, x_up, x_down = at_ten(x, 1 - core), at_ten(x + 1, core), at_ten(x - 1, core)

    barrier = pltpu.get_barrier_semaphore()
    peers = (up, down, right, left, sibling, x_up, x_down)
    for peer in peers:
        pl.semaphore_signal(barrier, inc=1, device_id=peer, device_id_type=MESH)

    w_copy = pltpu.make_async_copy(w_hbm, w, w_sem)
    w_copy.start()

    picks = picks_ref[...].reshape(1, CAP)
    count = jnp.sum(jnp.where(picks < TOK_DEV, 1.0, 0.0), axis=1, keepdims=True)
    row_id = lax.broadcasted_iota(jnp.int32, (CAP, HD), 0)
    valid = row_id.astype(jnp.float32) < count
    k_all, v_all = k_ref[...], v_ref[...]
    own[:, :HD] = jnp.where(valid, k_all.astype(jnp.float32), k_all[:1].astype(jnp.float32)).astype(jnp.bfloat16)
    own[:, HD:] = jnp.where(valid, v_all.astype(jnp.float32), FILL).astype(jnp.bfloat16)

    def place(name):
        return held.at[pl.ds(PLACE[name], ROWS[part_of(name)]), :]

    def own_part(part):
        return own.at[pl.ds(FIRST[part], ROWS[part]), :]

    def own_row(offset):
        if offset == 0:
            return own_part("A")
        name = ("ZL", "A", offset) if 0 < offset < 4 else ("ZR", "A", -offset if offset < 0 else 4)
        return place(name)

    def source(name):
        kind = name[0]
        if kind in ("ZR", "ZL"):
            _, stream, step = name
            target = right if kind == "ZR" else left
            if step > 1:
                return place((kind, stream, step - 1)), target
            if stream in ("A", "B0"):
                return own_part(stream[0]), target
            return place(("YB", {"Bm": "P", "Bp": "M", "B2": "2"}[stream])), target
        if kind == "YB":
            return (place(("YB", "P")) if name[1] == "2" else own_part("B")), (down if name[1] == "M" else up)
        if kind == "YP":
            return own_row(name[1]), up
        if kind == "YM":
            return own_row(name[1]), down
        if kind == "YP2":
            return place(("YP", name[1])), up
        return place(("YM", name[1])), down

    def shard(name):
        kind = name[0]
        if kind in ("ZR", "ZL"):
            return wrap(y + ROW_OF[name[1]], NY), wrap(z - name[2] if kind == "ZR" else z + name[2], NZ)
        if kind == "YB":
            return wrap(y + {"P": -1, "M": 1, "2": 2}[name[1]], NY), z
        return wrap(y + {"YP": -1, "YM": 1, "YP2": 2, "YM2": 2}[kind], NY), wrap(z + name[1], NZ)

    def transfer(name):
        i = NUMBER[name]
        src, target = source(name)
        return pltpu.make_async_remote_copy(
            src, place(name), send_sem.at[i], recv_sem.at[i], device_id=target, device_id_type=MESH
        )

    def start(name):
        transfer(name).start()

    def open_ring(stream):
        start(("ZR", stream, 1))
        start(("ZL", stream, 1))

    def open_column(offset):
        start(("YP", offset))
        start(("YM", offset))

    def arrive(name):
        transfer(name).wait_recv()
        kind = name[0]
        if kind in ("ZR", "ZL"):
            _, stream, step = name
            if step < TURNS[stream][0 if kind == "ZR" else 1]:
                start((kind, stream, step + 1))
            if stream == "A":
                open_column(step if kind == "ZL" else (-step if step < 4 else 4))
        elif kind == "YP" and name[1] in UPWARDS:
            start(("YP2", name[1]))
        elif kind == "YM" and name[1] not in UPWARDS:
            start(("YM2", name[1]))
        elif name == ("YB", "P"):
            start(("YB", "2"))
        for stream in OPENS.get(name, ()):
            open_ring(stream)

    def qk(g, half, keys):
        q = q_ref[half * TILE : (half + 1) * TILE, g * HD : (g + 1) * HD]
        return lax.dot_general(q, keys, (((1,), (1,)), ((), ())), preferred_element_type=jnp.float32)

    def tile(g, half):
        return pl.ds((half * GROUP + g) * TILE, TILE)

    def diagonal():
        va[:CAP, :HD] = v_ref[...]
        va[:CAP, HD:] = jnp.ones((CAP, HD), jnp.bfloat16)
        for half, g in ((0, 0), (0, 1), (0, 2), (0, 3), (1, 0), (1, 1), (1, 2), (1, 3)):
            rows = tile(g, half)
            scores = qk(g, half, k_ref[...])
            i = lax.broadcasted_iota(jnp.int32, scores.shape, 0) + half * TILE
            j = lax.broadcasted_iota(jnp.int32, scores.shape, 1)
            scores = jnp.where(j <= i, scores, NEG)
            top = jnp.max(scores, axis=1, keepdims=True)
            weights = jnp.exp2((scores - top) * KAPPA).astype(jnp.bfloat16)
            acc[rows, :] = jnp.dot(weights, va[:CAP, :], preferred_element_type=jnp.float32)
            row_max[rows, :] = jnp.broadcast_to(top, (TILE, HD))

    def unit(u, halves=(0, 1)):
        n = UNIT_ROWS[u]
        here = pl.ds(PLACE[UNITS[u][0]], n)
        seen = []
        for name in UNITS[u]:
            yy, zz = shard(name)
            seen.append(jnp.logical_or(yy < y, jnp.logical_and(yy == y, zz < z)))
        some = seen[0]
        for other in seen[1:]:
            some = jnp.logical_or(some, other)

        @pl.when(some)
        def _():
            if 0 in halves:
                block = held[here, HD:]
                real = block < FILL / 2
                va[:n, :HD] = jnp.where(real, block, 0).astype(jnp.bfloat16)
                va[:n, HD:] = jnp.where(real, 1, 0).astype(jnp.bfloat16)
            column = lax.broadcasted_iota(jnp.int32, (1, n), 1)
            hide = jnp.zeros((1, n), jnp.float32)
            for name, shown in zip(UNITS[u], seen):
                first = PLACE[name] - PLACE[UNITS[u][0]]
                inside = jnp.logical_and(column >= first, column < first + ROWS[part_of(name)])
                hide = jnp.where(inside, jnp.where(shown, 0.0, NEG), hide)
            for half, g in ((h, g) for h in halves for g in range(GROUP)):
                rows = tile(g, half)
                scores = qk(g, half, held[here, :HD]) + hide
                old = row_max[rows, :]
                new = jnp.maximum(old, jnp.max(scores, axis=1, keepdims=True))
                weights = jnp.exp2((scores - new[:, :1]) * KAPPA).astype(jnp.bfloat16)
                factor = jnp.exp2((old - new) * KAPPA)
                more = jnp.dot(weights, va[:n, :], preferred_element_type=jnp.float32)
                acc[rows, :HD] = acc[rows, :HD] * factor + more[:, :HD]
                acc[rows, HD:] = acc[rows, HD:] * factor + more[:, HD:]
                row_max[rows, :] = new

    def normalize(half):
        for g in range(GROUP):
            rows = tile(g, half)
            att[half * TILE : (half + 1) * TILE, g * HD : (g + 1) * HD] = (
                acc[rows, :HD] / acc[rows, HD:]
            ).astype(jnp.bfloat16)

    def block_rows(b):
        return pl.ds(b * TILE, TILE)

    def partial(d, cc, b):
        cols = pl.ds(pl.multiple_of((wrap(x + d, NX) * 2 + cc) * WIDTH, 128), WIDTH)
        return jnp.dot(att[block_rows(b), :], w[:, cols], preferred_element_type=jnp.float32)

    def to_sibling(d, b):
        i = 2 * d + b
        return pltpu.make_async_remote_copy(
            sib_out.at[d, block_rows(b)], sib_in.at[d, block_rows(b)], sib_send.at[i], sib_recv.at[i],
            device_id=sibling, device_id_type=MESH,
        )

    def x_copy(kind, way, b):
        i = (kind * 2 + way) * 2 + b
        first, count_rows = BLOCKS[b][way if kind < 2 else 1 - way]
        rows = pl.ds(first, count_rows)
        if kind == 0:
            src, dst = hop_out.at[rows], hop_in.at[rows]
        else:
            src, dst = end_out.at[way, rows], end_in.at[way, rows]
        return pltpu.make_async_remote_copy(
            src, dst, x_send.at[i], x_recv.at[i], device_id=(x_up, x_down)[way], device_id_type=MESH
        )

    def send_sibling(d, b):
        sib_out[d, block_rows(b)] = partial(d, 1 - core, b).astype(jnp.bfloat16)
        to_sibling(d, b).start()

    def chip_sum(d, b):
        mine = partial(d, core, b)
        to_sibling(d, b).wait_recv()
        return mine + sib_in[d, block_rows(b)].astype(jnp.float32)

    def far(b):
        send_sibling(2, b)
        send_sibling(1, b)
        hop_out[block_rows(b), :] = chip_sum(2, b).astype(jnp.bfloat16)
        x_copy(0, 0, b).start()
        x_copy(0, 1, b).start()
        send_sibling(3, b)

    def near(b):
        for way, d in ((0, 1), (1, 3)):
            total[way, block_rows(b)] = chip_sum(d, b)
            first, count_rows = BLOCKS[b][1 - way]
            rows = pl.ds(first, count_rows)
            end_out[way, rows] = total[way, rows].astype(jnp.bfloat16)
            x_copy(2, way, b).start()
        send_sibling(0, b)

    def pass_on(b):
        for way in (0, 1):
            first, count_rows = BLOCKS[b][way]
            rows = pl.ds(first, count_rows)
            x_copy(0, way, b).wait_recv()
            end_out[way, rows] = (total[way, rows] + hop_in[rows, :].astype(jnp.float32)).astype(jnp.bfloat16)
            x_copy(1, way, b).start()

    def finish(b):
        rows = block_rows(b)
        total[0, rows] = chip_sum(0, b)
        for way in (0, 1):
            here = pl.ds(*BLOCKS[b][way])
            x_copy(2, 1 - way, b).wait_recv()
            x_copy(1, way, b).wait_recv()
            projected = total[0, here] + end_in[0, here].astype(jnp.float32) + end_in[1, here].astype(jnp.float32)
            residual = stream_ref[here, :].astype(jnp.float32)
            inside = slice(BLOCKS[b][way][0], sum(BLOCKS[b][way]))
            updated = jnp.where(wide_valid[inside], residual + gain[inside] * projected, residual)
            out_ref[here, :] = updated.astype(jnp.bfloat16)

    pl.semaphore_wait(barrier, len(peers))
    for what in FIRST_SENDS:
        if what == "YB":
            start(("YB", "P"))
            start(("YB", "M"))
        elif what == "YA":
            open_column(0)
        else:
            open_ring(what)

    for what, *rest in ORDER[:-1]:
        if what == "w":
            arrive(tuple(rest))
        elif rest[0] == "diag":
            diagonal()
        else:
            unit(rest[0])

    unit(ORDER[-1][1], (0,))
    normalize(0)
    w_copy.wait()
    far(0)
    unit(ORDER[-1][1], (1,))
    normalize(1)
    near(0)
    far(1)
    pass_on(0)
    near(1)
    pass_on(1)

    router = router_ref[...].reshape(1, CAP)
    eye = lax.broadcasted_iota(jnp.int32, (CAP, CAP), 0) == lax.broadcasted_iota(jnp.int32, (CAP, CAP), 1)
    gain = jnp.sum(jnp.where(eye, router, 0.0), axis=1, keepdims=True)
    wide_valid = lax.broadcasted_iota(jnp.int32, (CAP, WIDTH), 0).astype(jnp.float32) < count
    finish(0)
    finish(1)

    for name in G_IDS:
        transfer(name).wait_send()
    for b in (0, 1):
        for d in range(NX):
            to_sibling(d, b).wait_send()
        for kind in range(3):
            for way in (0, 1):
                x_copy(kind, way, b).wait_send()


def local(stream_rows, picks, router, queries, keys, values, out_weight):
    vmem = pl.BlockSpec(memory_space=pltpu.VMEM)
    bf16, f32 = jnp.bfloat16, jnp.float32
    dma = pltpu.SemaphoreType.DMA
    return pl.pallas_call(
        kernel,
        out_shape=jax.ShapeDtypeStruct(stream_rows.shape, bf16),
        in_specs=[vmem] * 6 + [pl.BlockSpec(memory_space=pl.ANY)],
        out_specs=vmem,
        scratch_shapes=[
            pltpu.VMEM((CAP, 2 * HD), bf16),
            pltpu.VMEM((sum(UNIT_ROWS), 2 * HD), bf16),
            pltpu.VMEM((max(UNIT_ROWS), 2 * HD), bf16),
            pltpu.VMEM((GROUP * CAP, HD), f32),
            pltpu.VMEM((GROUP * CAP, 2 * HD), f32),
            pltpu.VMEM(out_weight.shape, bf16),
            pltpu.VMEM((CAP, GROUP * HD), bf16),
            pltpu.VMEM((NX, CAP, WIDTH), bf16),
            pltpu.VMEM((NX, CAP, WIDTH), bf16),
            pltpu.VMEM((CAP, WIDTH), bf16),
            pltpu.VMEM((CAP, WIDTH), bf16),
            pltpu.VMEM((2, CAP, WIDTH), bf16),
            pltpu.VMEM((2, CAP, WIDTH), bf16),
            pltpu.VMEM((2, CAP, WIDTH), f32),
            dma((N_GATHER,)),
            dma((N_GATHER,)),
            dma((2 * NX,)),
            dma((2 * NX,)),
            dma((12,)),
            dma((12,)),
            dma,
        ],
        compiler_params=pltpu.CompilerParams(
            collective_id=0, has_side_effects=True, vmem_limit_bytes=56 * 2**20
        ),
        cost_estimate=pl.CostEstimate(flops=8 * 10**9, bytes_accessed=10**7, transcendentals=10**7),
    )(queries, keys, values, picks, router, stream_rows, out_weight)


def solution(mesh):
    placed = (
        P("context", "tensor"),
        P("context"),
        P("context"),
        P("context", "tensor"),
        P("context", "tensor"),
        P("context", "tensor"),
        P("tensor", None),
    )
    return jax.shard_map(
        local, mesh=mesh, in_specs=placed, out_specs=P("context", "tensor"), check_vma=False
    )
```

```python
import jax
import jax.numpy as jnp
from jax import lax
from jax.experimental import pallas as pl
from jax.experimental.pallas import tpu as pltpu
from jax.sharding import PartitionSpec as P

MESH = pl.DeviceIdType.MESH

TOK_DEV = 1536
CAP = 288
HD = 128
NY, NZ, NX = 4, 8, 4
WIDTH = 896
GROUP = 4
KAPPA = 128**-0.5 * 1.4426950408889634
NEG = -1e30
FILL = 64.0
TILE = 144
VROWS = 144
ALL_COLS = ((0, 384), (384, 384), (768, 384))
LOW_COLS = ((0, 384), (384, 256))
HIGH_COLS = ((640, 512),)

ROWS = {"A": 176, "B": 112}
FIRST = {"A": 0, "B": 176}
TURNS = {"A": (4, 3), "B0": (4, 3), "Bm": (3, 4), "Bp": (3, 4), "B2": (3, 4)}
ROW_OF = {"A": 0, "B0": 0, "Bm": 3, "Bp": 1, "B2": 2}
OFFSETS = (0, -1, -2, -3, 4, 1, 2, 3)
UPWARDS = (0, -1, -2, -3)
FIRST_SENDS = ("A", "YB", "YA", "B0")
UNITS = (
    (("ZR", "A", 1), ("ZL", "A", 1), ("YP", 0), ("YB", "P"), ("YB", "M"), ("ZR", "B0", 1), ("ZL", "B0", 1),),
    (("YM", 0), ("ZR", "A", 2), ("YM", -1), ("ZL", "A", 2),),
    (("YP", -1), ("YM", 1), ("YP", 1), ("YB", "2"), ("ZR", "B0", 2),),
    (("YP2", 0), ("ZR", "A", 3), ("YM", -2), ("ZL", "B0", 2), ("ZL", "Bm", 1),),
    (("ZL", "A", 3), ("YP", -2), ("YM", 2), ("ZR", "Bm", 1), ("ZR", "Bp", 1),),
    (("YP", 2), ("ZL", "Bp", 1), ("ZR", "B0", 3), ("ZL", "B0", 3), ("ZR", "B2", 1), ("ZL", "B2", 1),),
    (("YM2", 1), ("YP2", -1), ("YM", -3), ("ZL", "Bm", 2), ("ZL", "Bp", 2),),
    (("ZR", "A", 4), ("YP", -3), ("YM", 3), ("YP", 3), ("YM2", 2), ("ZR", "Bm", 2),),
    (("YP2", -2), ("YM", 4), ("ZL", "B2", 2), ("ZR", "Bp", 2), ("ZR", "B0", 4), ("ZL", "Bm", 3), ("ZR", "B2", 2), ("ZL", "Bp", 3),),
    (("YP", 4), ("YM2", 3), ("YP2", -3), ("ZR", "Bm", 3), ("ZL", "B2", 3),),
    (("YM2", 4), ("ZR", "Bp", 3), ("ZL", "Bm", 4), ("ZR", "B2", 3),),
    (("ZL", "Bp", 4), ("ZL", "B2", 4),),
)
ORDER = (
    ("c", "diag"), ("w", "YB", "P"), ("w", "YB", "M"), ("w", "ZR", "A", 1), ("w", "ZL", "A", 1),
    ("w", "YP", 0), ("w", "YM", 0), ("w", "ZR", "B0", 1), ("w", "ZL", "B0", 1), ("c", 0), ("w", "YB", "2"),
    ("w", "ZR", "A", 2), ("w", "YM", -1), ("w", "ZL", "A", 2), ("c", 1), ("w", "YP", -1), ("w", "ZR", "B0", 2),
    ("w", "ZL", "B0", 2), ("w", "YM", 1), ("w", "YP", 1), ("c", 2), ("w", "ZL", "Bm", 1), ("w", "YP2", 0),
    ("w", "ZR", "A", 3), ("w", "YM", -2), ("c", 3), ("w", "ZR", "Bm", 1), ("w", "ZL", "A", 3), ("w", "YP", -2),
    ("w", "YM", 2), ("w", "ZR", "Bp", 1), ("w", "ZL", "Bp", 1), ("c", 4), ("w", "ZR", "B0", 3),
    ("w", "ZL", "B0", 3), ("w", "YP", 2), ("w", "YM2", 1), ("w", "ZR", "B2", 1), ("w", "ZL", "B2", 1), ("c", 5),
    ("w", "YP2", -1), ("w", "YM", -3), ("w", "ZL", "Bm", 2), ("w", "ZR", "A", 4), ("w", "ZL", "Bp", 2), ("c", 6),
    ("w", "YP", -3), ("w", "YM", 3), ("w", "ZR", "Bm", 2), ("w", "ZL", "B2", 2), ("w", "ZR", "Bp", 2),
    ("w", "YP", 3), ("w", "YM2", 2), ("c", 7), ("w", "ZR", "B0", 4), ("w", "ZL", "Bm", 3), ("w", "YP2", -2),
    ("w", "YM", 4), ("w", "ZR", "B2", 2), ("w", "ZL", "Bp", 3), ("c", 8), ("w", "ZR", "Bm", 3),
    ("w", "ZL", "B2", 3), ("w", "YP", 4), ("w", "YM2", 3), ("w", "ZR", "Bp", 3), ("w", "YP2", -3), ("c", 9),
    ("w", "ZL", "Bm", 4), ("w", "ZR", "B2", 3), ("w", "YM2", 4), ("w", "ZL", "Bp", 4), ("c", 10),
    ("w", "ZL", "B2", 4), ("c", 11),
)
OPENS = {
    ("ZR", "A", 2): ("Bm",),
    ("ZL", "A", 2): ("Bp",),
    ("ZL", "B0", 2): ("B2",),
}

Z_IDS = [(side, s, i + 1) for s, (r, l) in TURNS.items() for side, n in (("ZR", r), ("ZL", l)) for i in range(n)]
Y_IDS = [(kind, o) for kind in ("YP", "YM") for o in OFFSETS]
Y_IDS += [("YP2", o) for o in UPWARDS] + [("YM2", o) for o in OFFSETS if o not in UPWARDS]
Y_IDS += [("YB", "P"), ("YB", "M"), ("YB", "2")]
G_IDS = Z_IDS + Y_IDS
N_GATHER = len(G_IDS)
NUMBER = {name: i for i, name in enumerate(G_IDS)}


def part_of(name):
    return "A" if name[1] == "A" or (name[0][0] == "Y" and name[0] != "YB") else "B"


PLACE, UNIT_ROWS = {}, []
for unit_pieces in UNITS:
    begin = sum(UNIT_ROWS)
    end = begin
    for piece in unit_pieces:
        PLACE[piece] = end
        end += ROWS[part_of(piece)]
    UNIT_ROWS.append(end - begin)

BLOCKS = (((0, 80), (80, 64)), ((144, 64), (208, 80)))


def kernel(
    q_ref, k_ref, v_ref, picks_ref, router_ref, stream_ref, w_hbm, out_ref,
    own, held, stacked, vt, top, acc, w, att, sib_out, sib_in, hop_out, hop_in, end_out, end_in, total,
    send_sem, recv_sem, sib_send, sib_recv, x_send, x_recv, w_sem,
):
    ctx, ten = lax.axis_index("context"), lax.axis_index("tensor")
    y, z = ctx // NZ, lax.rem(ctx, NZ)
    x, core = ten // 2, lax.rem(ten, 2)

    def wrap(i, n):
        return lax.rem(i + 2 * n, n)

    def at_ctx(yy, zz):
        return (wrap(yy, NY) * NZ + wrap(zz, NZ), ten)

    def at_ten(xx, cc):
        return (ctx, wrap(xx, NX) * 2 + cc)

    up, down, right, left = at_ctx(y + 1, z), at_ctx(y - 1, z), at_ctx(y, z + 1), at_ctx(y, z - 1)
    sibling, x_up, x_down = at_ten(x, 1 - core), at_ten(x + 1, core), at_ten(x - 1, core)

    barrier = pltpu.get_barrier_semaphore()
    peers = (up, down, right, left, sibling, x_up, x_down)
    for peer in peers:
        pl.semaphore_signal(barrier, inc=1, device_id=peer, device_id_type=MESH)

    w_copy = pltpu.make_async_copy(w_hbm, w, w_sem)
    w_copy.start()

    picks = picks_ref[...].reshape(1, CAP)
    count = jnp.sum(jnp.where(picks < TOK_DEV, 1.0, 0.0), axis=1, keepdims=True)
    row_id = lax.broadcasted_iota(jnp.int32, (CAP, HD), 0)
    valid = row_id.astype(jnp.float32) < count
    k_all, v_all = k_ref[...], v_ref[...]
    own[:, :HD] = jnp.where(valid, k_all.astype(jnp.float32), k_all[:1].astype(jnp.float32)).astype(jnp.bfloat16)
    own[:, HD:] = jnp.where(valid, v_all.astype(jnp.float32), FILL).astype(jnp.bfloat16)

    def place(name):
        return held.at[pl.ds(PLACE[name], ROWS[part_of(name)]), :]

    def own_part(part):
        return own.at[pl.ds(FIRST[part], ROWS[part]), :]

    def own_row(offset):
        if offset == 0:
            return own_part("A")
        name = ("ZL", "A", offset) if 0 < offset < 4 else ("ZR", "A", -offset if offset < 0 else 4)
        return place(name)

    def source(name):
        kind = name[0]
        if kind in ("ZR", "ZL"):
            _, stream, step = name
            target = right if kind == "ZR" else left
            if step > 1:
                return place((kind, stream, step - 1)), target
            if stream in ("A", "B0"):
                return own_part(stream[0]), target
            return place(("YB", {"Bm": "P", "Bp": "M", "B2": "2"}[stream])), target
        if kind == "YB":
            return (place(("YB", "P")) if name[1] == "2" else own_part("B")), (down if name[1] == "M" else up)
        if kind == "YP":
            return own_row(name[1]), up
        if kind == "YM":
            return own_row(name[1]), down
        if kind == "YP2":
            return place(("YP", name[1])), up
        return place(("YM", name[1])), down

    def shard(name):
        kind = name[0]
        if kind in ("ZR", "ZL"):
            return wrap(y + ROW_OF[name[1]], NY), wrap(z - name[2] if kind == "ZR" else z + name[2], NZ)
        if kind == "YB":
            return wrap(y + {"P": -1, "M": 1, "2": 2}[name[1]], NY), z
        return wrap(y + {"YP": -1, "YM": 1, "YP2": 2, "YM2": 2}[kind], NY), wrap(z + name[1], NZ)

    def transfer(name):
        i = NUMBER[name]
        src, target = source(name)
        return pltpu.make_async_remote_copy(
            src, place(name), send_sem.at[i], recv_sem.at[i], device_id=target, device_id_type=MESH
        )

    def start(name):
        transfer(name).start()

    def open_ring(stream):
        start(("ZR", stream, 1))
        start(("ZL", stream, 1))

    def open_column(offset):
        start(("YP", offset))
        start(("YM", offset))

    def arrive(name):
        transfer(name).wait_recv()
        kind = name[0]
        if kind in ("ZR", "ZL"):
            _, stream, step = name
            if step < TURNS[stream][0 if kind == "ZR" else 1]:
                start((kind, stream, step + 1))
            if stream == "A":
                open_column(step if kind == "ZL" else (-step if step < 4 else 4))
        elif kind == "YP" and name[1] in UPWARDS:
            start(("YP2", name[1]))
        elif kind == "YM" and name[1] not in UPWARDS:
            start(("YM2", name[1]))
        elif name == ("YB", "P"):
            start(("YB", "2"))
        for stream in OPENS.get(name, ()):
            open_ring(stream)

    def tile(g, half):
        return pl.ds((half * GROUP + g) * TILE, TILE)

    def stack_queries():
        for half in (0, 1):
            for g in range(GROUP):
                stacked[tile(g, half), :] = q_ref[half * TILE : (half + 1) * TILE, g * HD : (g + 1) * HD]

    def qk(keys, cols):
        return lax.dot_general(
            keys, stacked[cols, :], (((1,), (1,)), ((), ())), preferred_element_type=jnp.float32
        )

    def diagonal():
        vt[:HD, :CAP] = jnp.transpose(v_ref[...])
        vt[HD:, :CAP] = jnp.ones((VROWS - HD, CAP), jnp.bfloat16)
        for first, width in ALL_COLS:
            cols = pl.ds(first, width)
            scores = qk(k_ref[...], cols)
            c = lax.broadcasted_iota(jnp.int32, (1, width), 1) + first
            i = jnp.where(c >= GROUP * TILE, TILE, 0) + lax.rem(c, TILE)
            j = lax.broadcasted_iota(jnp.int32, scores.shape, 0)
            scores = jnp.where(j <= i, scores, NEG)
            high = jnp.max(scores, axis=0, keepdims=True)
            weights = jnp.exp2((scores - high) * KAPPA).astype(jnp.bfloat16)
            acc[:, cols] = jnp.dot(vt[:, :CAP], weights, preferred_element_type=jnp.float32)
            top[:, cols] = jnp.broadcast_to(high, (8, width))

    def unit(u, columns=ALL_COLS, fill=True):
        n = UNIT_ROWS[u]
        here = pl.ds(PLACE[UNITS[u][0]], n)
        seen = []
        for name in UNITS[u]:
            yy, zz = shard(name)
            seen.append(jnp.logical_or(yy < y, jnp.logical_and(yy == y, zz < z)))
        some = seen[0]
        for other in seen[1:]:
            some = jnp.logical_or(some, other)

        @pl.when(some)
        def _():
            if fill:
                block = jnp.transpose(held[here, HD:])
                real = block < FILL / 2
                vt[:HD, :n] = jnp.where(real, block, 0).astype(jnp.bfloat16)
                vt[HD:, :n] = jnp.where(real[: VROWS - HD], 1, 0).astype(jnp.bfloat16)
            hide = [jnp.where(shown, 0.0, NEG) for shown in seen]

            def score(cols):
                raw = qk(held[here, :HD], cols)
                parts, first = [], 0
                for name, shift in zip(UNITS[u], hide):
                    rows = ROWS[part_of(name)]
                    parts.append(raw[first : first + rows] + shift)
                    first += rows
                return jnp.concatenate(parts, axis=0)

            def soften(cols, scores):
                old = top[:, cols]
                new = jnp.maximum(old, jnp.max(scores, axis=0, keepdims=True))
                top[:, cols] = new
                return jnp.exp2((scores - new[:1]) * KAPPA).astype(jnp.bfloat16), jnp.exp2((old - new) * KAPPA)

            def mix(cols, weights, factor):
                more = jnp.dot(vt[:, :n], weights, preferred_element_type=jnp.float32)
                acc[:, cols] = acc[:, cols] * factor[:1] + more

            spans = [pl.ds(*span) for span in columns]
            scores, waiting = score(spans[0]), None
            for at, cols in enumerate(spans):
                following = score(spans[at + 1]) if at + 1 < len(spans) else None
                softened = soften(cols, scores)
                if waiting is not None:
                    mix(*waiting)
                waiting, scores = (cols, *softened), following
            mix(*waiting)

    def normalize(half):
        first, width = ((0, 640), (512, 640))[half]
        cols = pl.ds(first, width)
        flat = jnp.transpose(acc[:HD, cols] / acc[HD : HD + 1, cols]).astype(jnp.bfloat16)
        for g in range(GROUP):
            start_row = (half * GROUP + g) * TILE - first
            att[half * TILE : (half + 1) * TILE, g * HD : (g + 1) * HD] = flat[start_row : start_row + TILE]

    def block_rows(b):
        return pl.ds(b * TILE, TILE)

    def partial(d, cc, b):
        cols = pl.ds(pl.multiple_of((wrap(x + d, NX) * 2 + cc) * WIDTH, 128), WIDTH)
        return jnp.dot(att[block_rows(b), :], w[:, cols], preferred_element_type=jnp.float32)

    def to_sibling(d, b):
        i = 2 * d + b
        return pltpu.make_async_remote_copy(
            sib_out.at[d, block_rows(b)], sib_in.at[d, block_rows(b)], sib_send.at[i], sib_recv.at[i],
            device_id=sibling, device_id_type=MESH,
        )

    def x_copy(kind, way, b):
        i = (kind * 2 + way) * 2 + b
        first, count_rows = BLOCKS[b][way if kind < 2 else 1 - way]
        rows = pl.ds(first, count_rows)
        if kind == 0:
            src, dst = hop_out.at[rows], hop_in.at[rows]
        else:
            src, dst = end_out.at[way, rows], end_in.at[way, rows]
        return pltpu.make_async_remote_copy(
            src, dst, x_send.at[i], x_recv.at[i], device_id=(x_up, x_down)[way], device_id_type=MESH
        )

    def send_sibling(d, b):
        sib_out[d, block_rows(b)] = partial(d, 1 - core, b).astype(jnp.bfloat16)
        to_sibling(d, b).start()

    def chip_sum(d, b):
        mine = partial(d, core, b)
        to_sibling(d, b).wait_recv()
        return mine + sib_in[d, block_rows(b)].astype(jnp.float32)

    def far(b):
        send_sibling(2, b)
        send_sibling(1, b)
        hop_out[block_rows(b), :] = chip_sum(2, b).astype(jnp.bfloat16)
        x_copy(0, 0, b).start()
        x_copy(0, 1, b).start()
        send_sibling(3, b)

    def near(b):
        for way, d in ((0, 1), (1, 3)):
            total[way, block_rows(b)] = chip_sum(d, b)
            first, count_rows = BLOCKS[b][1 - way]
            rows = pl.ds(first, count_rows)
            end_out[way, rows] = total[way, rows].astype(jnp.bfloat16)
            x_copy(2, way, b).start()
        send_sibling(0, b)

    def pass_on(b):
        for way in (0, 1):
            first, count_rows = BLOCKS[b][way]
            rows = pl.ds(first, count_rows)
            x_copy(0, way, b).wait_recv()
            end_out[way, rows] = (total[way, rows] + hop_in[rows, :].astype(jnp.float32)).astype(jnp.bfloat16)
            x_copy(1, way, b).start()

    def finish(b):
        rows = block_rows(b)
        total[0, rows] = chip_sum(0, b)
        for way in (0, 1):
            here = pl.ds(*BLOCKS[b][way])
            x_copy(2, 1 - way, b).wait_recv()
            x_copy(1, way, b).wait_recv()
            projected = total[0, here] + end_in[0, here].astype(jnp.float32) + end_in[1, here].astype(jnp.float32)
            residual = stream_ref[here, :].astype(jnp.float32)
            inside = slice(BLOCKS[b][way][0], sum(BLOCKS[b][way]))
            updated = jnp.where(wide_valid[inside], residual + gain[inside] * projected, residual)
            out_ref[here, :] = updated.astype(jnp.bfloat16)

    stack_queries()
    pl.semaphore_wait(barrier, len(peers))
    for what in FIRST_SENDS:
        if what == "YB":
            start(("YB", "P"))
            start(("YB", "M"))
        elif what == "YA":
            open_column(0)
        else:
            open_ring(what)

    for what, *rest in ORDER[:-1]:
        if what == "w":
            arrive(tuple(rest))
        elif rest[0] == "diag":
            diagonal()
        else:
            unit(rest[0])

    unit(ORDER[-1][1], LOW_COLS)
    normalize(0)
    w_copy.wait()
    far(0)
    unit(ORDER[-1][1], HIGH_COLS, False)
    normalize(1)
    near(0)
    far(1)
    pass_on(0)
    near(1)
    pass_on(1)

    router = router_ref[...].reshape(1, CAP)
    eye = lax.broadcasted_iota(jnp.int32, (CAP, CAP), 0) == lax.broadcasted_iota(jnp.int32, (CAP, CAP), 1)
    gain = jnp.sum(jnp.where(eye, router, 0.0), axis=1, keepdims=True)
    wide_valid = lax.broadcasted_iota(jnp.int32, (CAP, WIDTH), 0).astype(jnp.float32) < count
    for name in G_IDS:
        transfer(name).wait_send()
    for b in (0, 1):
        for d in range(NX):
            to_sibling(d, b).wait_send()
    finish(0)
    finish(1)
    for b in (0, 1):
        for kind in range(3):
            for way in (0, 1):
                x_copy(kind, way, b).wait_send()


def local(stream_rows, picks, router, queries, keys, values, out_weight):
    vmem = pl.BlockSpec(memory_space=pltpu.VMEM)
    bf16, f32 = jnp.bfloat16, jnp.float32
    dma = pltpu.SemaphoreType.DMA
    return pl.pallas_call(
        kernel,
        out_shape=jax.ShapeDtypeStruct(stream_rows.shape, bf16),
        in_specs=[vmem] * 6 + [pl.BlockSpec(memory_space=pl.ANY)],
        out_specs=vmem,
        scratch_shapes=[
            pltpu.VMEM((CAP, 2 * HD), bf16),
            pltpu.VMEM((sum(UNIT_ROWS), 2 * HD), bf16),
            pltpu.VMEM((GROUP * CAP, HD), bf16),
            pltpu.VMEM((VROWS, max(UNIT_ROWS)), bf16),
            pltpu.VMEM((8, GROUP * CAP), f32),
            pltpu.VMEM((VROWS, GROUP * CAP), f32),
            pltpu.VMEM(out_weight.shape, bf16),
            pltpu.VMEM((CAP, GROUP * HD), bf16),
            pltpu.VMEM((NX, CAP, WIDTH), bf16),
            pltpu.VMEM((NX, CAP, WIDTH), bf16),
            pltpu.VMEM((CAP, WIDTH), bf16),
            pltpu.VMEM((CAP, WIDTH), bf16),
            pltpu.VMEM((2, CAP, WIDTH), bf16),
            pltpu.VMEM((2, CAP, WIDTH), bf16),
            pltpu.VMEM((2, CAP, WIDTH), f32),
            dma((N_GATHER,)),
            dma((N_GATHER,)),
            dma((2 * NX,)),
            dma((2 * NX,)),
            dma((12,)),
            dma((12,)),
            dma,
        ],
        compiler_params=pltpu.CompilerParams(
            collective_id=0, has_side_effects=True, vmem_limit_bytes=56 * 2**20
        ),
        cost_estimate=pl.CostEstimate(flops=8 * 10**9, bytes_accessed=10**7, transcendentals=10**7),
    )(queries, keys, values, picks, router, stream_rows, out_weight)


def solution(mesh):
    placed = (
        P("context", "tensor"),
        P("context"),
        P("context"),
        P("context", "tensor"),
        P("context", "tensor"),
        P("context", "tensor"),
        P("tensor", None),
    )
    return jax.shard_map(
        local, mesh=mesh, in_specs=placed, out_specs=P("context", "tensor"), check_vma=False
    )
```

```python
import jax
import jax.numpy as jnp
from jax import lax
from jax.experimental import pallas as pl
from jax.experimental.pallas import tpu as pltpu
from jax.sharding import PartitionSpec as P

MESH = pl.DeviceIdType.MESH

TOK_DEV = 1536
CAP = 288
HD = 128
NY, NZ, NX = 4, 8, 4
WIDTH = 896
GROUP = 4
KAPPA = 128**-0.5 * 1.4426950408889634
NEG = -1e30
FILL = 64.0
TILE = 144
VROWS = 144
ALL_COLS = ((0, 384), (384, 384), (768, 384))
LOW_COLS = ((0, 384), (384, 256))
HIGH_COLS = ((640, 512),)

ROWS = {"A": 176, "B": 112}
FIRST = {"A": 0, "B": 176}
TURNS = {"A": (4, 3), "B0": (4, 3), "Bm": (3, 4), "Bp": (3, 4), "B2": (3, 4)}
ROW_OF = {"A": 0, "B0": 0, "Bm": 3, "Bp": 1, "B2": 2}
OFFSETS = (0, -1, -2, -3, 4, 1, 2, 3)
UPWARDS = (0, -1, -2, -3)
FIRST_SENDS = ("A", "YB", "YA", "B0")
UNITS = (
    (("ZR", "A", 1), ("ZL", "A", 1), ("YP", 0), ("YB", "P"), ("YB", "M"), ("ZR", "B0", 1), ("ZL", "B0", 1),),
    (("YM", 0), ("ZR", "A", 2), ("YM", -1), ("ZL", "A", 2),),
    (("YP", -1), ("YM", 1), ("YP", 1), ("YB", "2"), ("ZR", "B0", 2),),
    (("YP2", 0), ("ZR", "A", 3), ("YM", -2), ("ZL", "B0", 2), ("ZL", "Bm", 1),),
    (("ZL", "A", 3), ("YP", -2), ("YM", 2), ("ZR", "Bm", 1), ("ZR", "Bp", 1),),
    (("YP", 2), ("ZL", "Bp", 1), ("ZR", "B0", 3), ("ZL", "B0", 3), ("ZR", "B2", 1), ("ZL", "B2", 1),),
    (("YM2", 1), ("YP2", -1), ("YM", -3), ("ZL", "Bm", 2), ("ZL", "Bp", 2),),
    (("ZR", "A", 4), ("YP", -3), ("YM", 3), ("YP", 3), ("YM2", 2), ("ZR", "Bm", 2),),
    (("YP2", -2), ("YM", 4), ("ZL", "B2", 2), ("ZR", "Bp", 2), ("ZR", "B0", 4), ("ZL", "Bm", 3), ("ZR", "B2", 2), ("ZL", "Bp", 3),),
    (("YP", 4), ("YM2", 3), ("YP2", -3), ("ZR", "Bm", 3), ("ZL", "B2", 3),),
    (("YM2", 4), ("ZR", "Bp", 3), ("ZL", "Bm", 4), ("ZR", "B2", 3),),
    (("ZL", "Bp", 4), ("ZL", "B2", 4),),
)
ORDER = (
    ("c", "diag"), ("w", "YB", "P"), ("w", "YB", "M"), ("w", "ZR", "A", 1), ("w", "ZL", "A", 1),
    ("w", "YP", 0), ("w", "YM", 0), ("w", "ZR", "B0", 1), ("w", "ZL", "B0", 1), ("c", 0), ("w", "YB", "2"),
    ("w", "ZR", "A", 2), ("w", "YM", -1), ("w", "ZL", "A", 2), ("c", 1), ("w", "YP", -1), ("w", "ZR", "B0", 2),
    ("w", "ZL", "B0", 2), ("w", "YM", 1), ("w", "YP", 1), ("c", 2), ("w", "ZL", "Bm", 1), ("w", "YP2", 0),
    ("w", "ZR", "A", 3), ("w", "YM", -2), ("c", 3), ("w", "ZR", "Bm", 1), ("w", "ZL", "A", 3), ("w", "YP", -2),
    ("w", "YM", 2), ("w", "ZR", "Bp", 1), ("w", "ZL", "Bp", 1), ("c", 4), ("w", "ZR", "B0", 3),
    ("w", "ZL", "B0", 3), ("w", "YP", 2), ("w", "YM2", 1), ("w", "ZR", "B2", 1), ("w", "ZL", "B2", 1), ("c", 5),
    ("w", "YP2", -1), ("w", "YM", -3), ("w", "ZL", "Bm", 2), ("w", "ZR", "A", 4), ("w", "ZL", "Bp", 2), ("c", 6),
    ("w", "YP", -3), ("w", "YM", 3), ("w", "ZR", "Bm", 2), ("w", "ZL", "B2", 2), ("w", "ZR", "Bp", 2),
    ("w", "YP", 3), ("w", "YM2", 2), ("c", 7), ("w", "ZR", "B0", 4), ("w", "ZL", "Bm", 3), ("w", "YP2", -2),
    ("w", "YM", 4), ("w", "ZR", "B2", 2), ("w", "ZL", "Bp", 3), ("c", 8), ("w", "ZR", "Bm", 3),
    ("w", "ZL", "B2", 3), ("w", "YP", 4), ("w", "YM2", 3), ("w", "ZR", "Bp", 3), ("w", "YP2", -3), ("c", 9),
    ("w", "ZL", "Bm", 4), ("w", "ZR", "B2", 3), ("w", "YM2", 4), ("w", "ZL", "Bp", 4), ("c", 10),
    ("w", "ZL", "B2", 4), ("c", 11),
)
OPENS = {
    ("ZR", "A", 2): ("Bm",),
    ("ZL", "A", 2): ("Bp",),
    ("ZL", "B0", 2): ("B2",),
}

Z_IDS = [(side, s, i + 1) for s, (r, l) in TURNS.items() for side, n in (("ZR", r), ("ZL", l)) for i in range(n)]
Y_IDS = [(kind, o) for kind in ("YP", "YM") for o in OFFSETS]
Y_IDS += [("YP2", o) for o in UPWARDS] + [("YM2", o) for o in OFFSETS if o not in UPWARDS]
Y_IDS += [("YB", "P"), ("YB", "M"), ("YB", "2")]
G_IDS = Z_IDS + Y_IDS
N_GATHER = len(G_IDS)
NUMBER = {name: i for i, name in enumerate(G_IDS)}


def part_of(name):
    return "A" if name[1] == "A" or (name[0][0] == "Y" and name[0] != "YB") else "B"


PLACE, UNIT_ROWS = {}, []
for unit_pieces in UNITS:
    begin = sum(UNIT_ROWS)
    end = begin
    for piece in unit_pieces:
        PLACE[piece] = end
        end += ROWS[part_of(piece)]
    UNIT_ROWS.append(end - begin)

BLOCKS = (((0, 80), (80, 64)), ((144, 64), (208, 80)))


def kernel(
    q_hbm, k_ref, v_ref, picks_ref, router_ref, stream_hbm, w_hbm, out_hbm, q_ref, stream_ref, out_ref,
    own, held, stacked, vt, top, acc, w, att, sib_out, sib_in, hop_out, hop_in, end_out, end_in, total,
    send_sem, recv_sem, sib_send, sib_recv, x_send, x_recv, w_sem, in_sems, out_sems,
):
    ctx, ten = lax.axis_index("context"), lax.axis_index("tensor")
    y, z = ctx // NZ, lax.rem(ctx, NZ)
    x, core = ten // 2, lax.rem(ten, 2)

    def wrap(i, n):
        return lax.rem(i + 2 * n, n)

    def at_ctx(yy, zz):
        return (wrap(yy, NY) * NZ + wrap(zz, NZ), ten)

    def at_ten(xx, cc):
        return (ctx, wrap(xx, NX) * 2 + cc)

    up, down, right, left = at_ctx(y + 1, z), at_ctx(y - 1, z), at_ctx(y, z + 1), at_ctx(y, z - 1)
    sibling, x_up, x_down = at_ten(x, 1 - core), at_ten(x + 1, core), at_ten(x - 1, core)

    barrier = pltpu.get_barrier_semaphore()
    peers = (up, down, right, left, sibling, x_up, x_down)
    for peer in peers:
        pl.semaphore_signal(barrier, inc=1, device_id=peer, device_id_type=MESH)

    w_copy = pltpu.make_async_copy(w_hbm, w, w_sem)
    q_copy = pltpu.make_async_copy(q_hbm, q_ref, in_sems.at[0])
    stream_copy = pltpu.make_async_copy(stream_hbm, stream_ref, in_sems.at[1])
    q_copy.start()
    stream_copy.start()
    w_copy.start()

    picks = picks_ref[...].reshape(1, CAP)
    count = jnp.sum(jnp.where(picks < TOK_DEV, 1.0, 0.0), axis=1, keepdims=True)
    row_id = lax.broadcasted_iota(jnp.int32, (CAP, HD), 0)
    valid = row_id.astype(jnp.float32) < count
    k_all, v_all = k_ref[...], v_ref[...]
    own[:, :HD] = jnp.where(valid, k_all.astype(jnp.float32), k_all[:1].astype(jnp.float32)).astype(jnp.bfloat16)
    own[:, HD:] = jnp.where(valid, v_all.astype(jnp.float32), FILL).astype(jnp.bfloat16)

    def place(name):
        return held.at[pl.ds(PLACE[name], ROWS[part_of(name)]), :]

    def own_part(part):
        return own.at[pl.ds(FIRST[part], ROWS[part]), :]

    def own_row(offset):
        if offset == 0:
            return own_part("A")
        name = ("ZL", "A", offset) if 0 < offset < 4 else ("ZR", "A", -offset if offset < 0 else 4)
        return place(name)

    def source(name):
        kind = name[0]
        if kind in ("ZR", "ZL"):
            _, stream, step = name
            target = right if kind == "ZR" else left
            if step > 1:
                return place((kind, stream, step - 1)), target
            if stream in ("A", "B0"):
                return own_part(stream[0]), target
            return place(("YB", {"Bm": "P", "Bp": "M", "B2": "2"}[stream])), target
        if kind == "YB":
            return (place(("YB", "P")) if name[1] == "2" else own_part("B")), (down if name[1] == "M" else up)
        if kind == "YP":
            return own_row(name[1]), up
        if kind == "YM":
            return own_row(name[1]), down
        if kind == "YP2":
            return place(("YP", name[1])), up
        return place(("YM", name[1])), down

    def shard(name):
        kind = name[0]
        if kind in ("ZR", "ZL"):
            return wrap(y + ROW_OF[name[1]], NY), wrap(z - name[2] if kind == "ZR" else z + name[2], NZ)
        if kind == "YB":
            return wrap(y + {"P": -1, "M": 1, "2": 2}[name[1]], NY), z
        return wrap(y + {"YP": -1, "YM": 1, "YP2": 2, "YM2": 2}[kind], NY), wrap(z + name[1], NZ)

    def transfer(name):
        i = NUMBER[name]
        src, target = source(name)
        return pltpu.make_async_remote_copy(
            src, place(name), send_sem.at[i], recv_sem.at[i], device_id=target, device_id_type=MESH
        )

    def start(name):
        transfer(name).start()

    def open_ring(stream):
        start(("ZR", stream, 1))
        start(("ZL", stream, 1))

    def open_column(offset):
        start(("YP", offset))
        start(("YM", offset))

    def arrive(name):
        transfer(name).wait_recv()
        kind = name[0]
        if kind in ("ZR", "ZL"):
            _, stream, step = name
            if step < TURNS[stream][0 if kind == "ZR" else 1]:
                start((kind, stream, step + 1))
            if stream == "A":
                open_column(step if kind == "ZL" else (-step if step < 4 else 4))
        elif kind == "YP" and name[1] in UPWARDS:
            start(("YP2", name[1]))
        elif kind == "YM" and name[1] not in UPWARDS:
            start(("YM2", name[1]))
        elif name == ("YB", "P"):
            start(("YB", "2"))
        for stream in OPENS.get(name, ()):
            open_ring(stream)

    def tile(g, half):
        return pl.ds((half * GROUP + g) * TILE, TILE)

    def stack_queries():
        for half in (0, 1):
            for g in range(GROUP):
                stacked[tile(g, half), :] = q_ref[half * TILE : (half + 1) * TILE, g * HD : (g + 1) * HD]

    def qk(keys, cols):
        return lax.dot_general(
            keys, stacked[cols, :], (((1,), (1,)), ((), ())), preferred_element_type=jnp.float32
        )

    def diagonal():
        vt[:HD, :CAP] = jnp.transpose(v_ref[...])
        vt[HD:, :CAP] = jnp.ones((VROWS - HD, CAP), jnp.bfloat16)
        for first, width in ALL_COLS:
            cols = pl.ds(first, width)
            scores = qk(k_ref[...], cols)
            c = lax.broadcasted_iota(jnp.int32, (1, width), 1) + first
            i = jnp.where(c >= GROUP * TILE, TILE, 0) + lax.rem(c, TILE)
            j = lax.broadcasted_iota(jnp.int32, scores.shape, 0)
            scores = jnp.where(j <= i, scores, NEG)
            high = jnp.max(scores, axis=0, keepdims=True)
            weights = jnp.exp2((scores - high) * KAPPA).astype(jnp.bfloat16)
            acc[:, cols] = jnp.dot(vt[:, :CAP], weights, preferred_element_type=jnp.float32)
            top[:, cols] = jnp.broadcast_to(high, (8, width))

    def unit(u, columns=ALL_COLS, fill=True):
        n = UNIT_ROWS[u]
        here = pl.ds(PLACE[UNITS[u][0]], n)
        seen = []
        for name in UNITS[u]:
            yy, zz = shard(name)
            seen.append(jnp.logical_or(yy < y, jnp.logical_and(yy == y, zz < z)))
        some = seen[0]
        for other in seen[1:]:
            some = jnp.logical_or(some, other)

        @pl.when(some)
        def _():
            if fill:
                block = jnp.transpose(held[here, HD:])
                real = block < FILL / 2
                vt[:HD, :n] = jnp.where(real, block, 0).astype(jnp.bfloat16)
                vt[HD:, :n] = jnp.where(real[: VROWS - HD], 1, 0).astype(jnp.bfloat16)
            hide = [jnp.where(shown, 0.0, NEG) for shown in seen]

            def score(cols):
                raw = qk(held[here, :HD], cols)
                parts, first = [], 0
                for name, shift in zip(UNITS[u], hide):
                    rows = ROWS[part_of(name)]
                    parts.append(raw[first : first + rows] + shift)
                    first += rows
                return jnp.concatenate(parts, axis=0)

            def soften(cols, scores):
                old = top[:, cols]
                new = jnp.maximum(old, jnp.max(scores, axis=0, keepdims=True))
                top[:, cols] = new
                return jnp.exp2((scores - new[:1]) * KAPPA).astype(jnp.bfloat16), jnp.exp2((old - new) * KAPPA)

            def mix(cols, weights, factor):
                more = jnp.dot(vt[:, :n], weights, preferred_element_type=jnp.float32)
                acc[:, cols] = acc[:, cols] * factor[:1] + more

            spans = [pl.ds(*span) for span in columns]
            scores, waiting = score(spans[0]), None
            for at, cols in enumerate(spans):
                following = score(spans[at + 1]) if at + 1 < len(spans) else None
                softened = soften(cols, scores)
                if waiting is not None:
                    mix(*waiting)
                waiting, scores = (cols, *softened), following
            mix(*waiting)

    def normalize(half):
        first, width = ((0, 640), (512, 640))[half]
        cols = pl.ds(first, width)
        flat = jnp.transpose(acc[:HD, cols] / acc[HD : HD + 1, cols]).astype(jnp.bfloat16)
        for g in range(GROUP):
            start_row = (half * GROUP + g) * TILE - first
            att[half * TILE : (half + 1) * TILE, g * HD : (g + 1) * HD] = flat[start_row : start_row + TILE]

    def block_rows(b):
        return pl.ds(b * TILE, TILE)

    def partial(d, cc, b):
        cols = pl.ds(pl.multiple_of((wrap(x + d, NX) * 2 + cc) * WIDTH, 128), WIDTH)
        return jnp.dot(att[block_rows(b), :], w[:, cols], preferred_element_type=jnp.float32)

    def to_sibling(d, b):
        i = 2 * d + b
        return pltpu.make_async_remote_copy(
            sib_out.at[d, block_rows(b)], sib_in.at[d, block_rows(b)], sib_send.at[i], sib_recv.at[i],
            device_id=sibling, device_id_type=MESH,
        )

    def x_copy(kind, way, b):
        i = (kind * 2 + way) * 2 + b
        first, count_rows = BLOCKS[b][way if kind < 2 else 1 - way]
        rows = pl.ds(first, count_rows)
        if kind == 0:
            src, dst = hop_out.at[rows], hop_in.at[rows]
        else:
            src, dst = end_out.at[way, rows], end_in.at[way, rows]
        return pltpu.make_async_remote_copy(
            src, dst, x_send.at[i], x_recv.at[i], device_id=(x_up, x_down)[way], device_id_type=MESH
        )

    def send_sibling(d, b):
        sib_out[d, block_rows(b)] = partial(d, 1 - core, b).astype(jnp.bfloat16)
        to_sibling(d, b).start()

    def chip_sum(d, b):
        mine = partial(d, core, b)
        to_sibling(d, b).wait_recv()
        return mine + sib_in[d, block_rows(b)].astype(jnp.float32)

    def far(b):
        send_sibling(2, b)
        send_sibling(1, b)
        hop_out[block_rows(b), :] = chip_sum(2, b).astype(jnp.bfloat16)
        x_copy(0, 0, b).start()
        x_copy(0, 1, b).start()
        send_sibling(3, b)

    def near(b):
        for way, d in ((0, 1), (1, 3)):
            total[way, block_rows(b)] = chip_sum(d, b)
            first, count_rows = BLOCKS[b][1 - way]
            rows = pl.ds(first, count_rows)
            end_out[way, rows] = total[way, rows].astype(jnp.bfloat16)
            x_copy(2, way, b).start()
        send_sibling(0, b)

    def pass_on(b):
        for way in (0, 1):
            first, count_rows = BLOCKS[b][way]
            rows = pl.ds(first, count_rows)
            x_copy(0, way, b).wait_recv()
            end_out[way, rows] = (total[way, rows] + hop_in[rows, :].astype(jnp.float32)).astype(jnp.bfloat16)
            x_copy(1, way, b).start()

    def out_copy(b, way):
        here = pl.ds(*BLOCKS[b][way])
        return pltpu.make_async_copy(out_ref.at[here], out_hbm.at[here], out_sems.at[2 * b + way])

    def finish(b):
        rows = block_rows(b)
        total[0, rows] = chip_sum(0, b)
        for way in (0, 1):
            here = pl.ds(*BLOCKS[b][way])
            x_copy(2, 1 - way, b).wait_recv()
            x_copy(1, way, b).wait_recv()
            projected = total[0, here] + end_in[0, here].astype(jnp.float32) + end_in[1, here].astype(jnp.float32)
            residual = stream_ref[here, :].astype(jnp.float32)
            inside = slice(BLOCKS[b][way][0], sum(BLOCKS[b][way]))
            updated = jnp.where(wide_valid[inside], residual + gain[inside] * projected, residual)
            out_ref[here, :] = updated.astype(jnp.bfloat16)
            out_copy(b, way).start()

    q_copy.wait()
    stack_queries()
    pl.semaphore_wait(barrier, len(peers))
    for what in FIRST_SENDS:
        if what == "YB":
            start(("YB", "P"))
            start(("YB", "M"))
        elif what == "YA":
            open_column(0)
        else:
            open_ring(what)

    for what, *rest in ORDER[:-1]:
        if what == "w":
            arrive(tuple(rest))
        elif rest[0] == "diag":
            diagonal()
        else:
            unit(rest[0])

    unit(ORDER[-1][1], LOW_COLS)
    normalize(0)
    w_copy.wait()
    far(0)
    unit(ORDER[-1][1], HIGH_COLS, False)
    normalize(1)
    near(0)
    far(1)
    pass_on(0)
    near(1)
    pass_on(1)

    router = router_ref[...].reshape(1, CAP)
    eye = lax.broadcasted_iota(jnp.int32, (CAP, CAP), 0) == lax.broadcasted_iota(jnp.int32, (CAP, CAP), 1)
    gain = jnp.sum(jnp.where(eye, router, 0.0), axis=1, keepdims=True)
    wide_valid = lax.broadcasted_iota(jnp.int32, (CAP, WIDTH), 0).astype(jnp.float32) < count
    for name in G_IDS:
        transfer(name).wait_send()
    for b in (0, 1):
        for d in range(NX):
            to_sibling(d, b).wait_send()
    stream_copy.wait()
    finish(0)
    finish(1)
    for b in (0, 1):
        for way in (0, 1):
            out_copy(b, way).wait()
    for b in (0, 1):
        for kind in range(3):
            for way in (0, 1):
                x_copy(kind, way, b).wait_send()


def local(stream_rows, picks, router, queries, keys, values, out_weight):
    vmem, anywhere = pl.BlockSpec(memory_space=pltpu.VMEM), pl.BlockSpec(memory_space=pl.ANY)
    bf16, f32 = jnp.bfloat16, jnp.float32
    dma = pltpu.SemaphoreType.DMA
    return pl.pallas_call(
        kernel,
        out_shape=jax.ShapeDtypeStruct(stream_rows.shape, bf16),
        in_specs=[anywhere] + [vmem] * 4 + [anywhere] * 2,
        out_specs=anywhere,
        scratch_shapes=[
            pltpu.VMEM(queries.shape, bf16),
            pltpu.VMEM(stream_rows.shape, bf16),
            pltpu.VMEM(stream_rows.shape, bf16),
            pltpu.VMEM((CAP, 2 * HD), bf16),
            pltpu.VMEM((sum(UNIT_ROWS), 2 * HD), bf16),
            pltpu.VMEM((GROUP * CAP, HD), bf16),
            pltpu.VMEM((VROWS, max(UNIT_ROWS)), bf16),
            pltpu.VMEM((8, GROUP * CAP), f32),
            pltpu.VMEM((VROWS, GROUP * CAP), f32),
            pltpu.VMEM(out_weight.shape, bf16),
            pltpu.VMEM((CAP, GROUP * HD), bf16),
            pltpu.VMEM((NX, CAP, WIDTH), bf16),
            pltpu.VMEM((NX, CAP, WIDTH), bf16),
            pltpu.VMEM((CAP, WIDTH), bf16),
            pltpu.VMEM((CAP, WIDTH), bf16),
            pltpu.VMEM((2, CAP, WIDTH), bf16),
            pltpu.VMEM((2, CAP, WIDTH), bf16),
            pltpu.VMEM((2, CAP, WIDTH), f32),
            dma((N_GATHER,)),
            dma((N_GATHER,)),
            dma((2 * NX,)),
            dma((2 * NX,)),
            dma((12,)),
            dma((12,)),
            dma,
            dma((2,)),
            dma((4,)),
        ],
        compiler_params=pltpu.CompilerParams(
            collective_id=0, has_side_effects=True, vmem_limit_bytes=56 * 2**20
        ),
        cost_estimate=pl.CostEstimate(flops=8 * 10**9, bytes_accessed=10**7, transcendentals=10**7),
    )(queries, keys, values, picks, router, stream_rows, out_weight)


def solution(mesh):
    placed = (
        P("context", "tensor"),
        P("context"),
        P("context"),
        P("context", "tensor"),
        P("context", "tensor"),
        P("context", "tensor"),
        P("tensor", None),
    )
    return jax.shard_map(
        local, mesh=mesh, in_specs=placed, out_specs=P("context", "tensor"), check_vma=False
    )
```

```python
import jax
import jax.numpy as jnp
from jax import lax
from jax.experimental import pallas as pl
from jax.experimental.pallas import tpu as pltpu
from jax.sharding import PartitionSpec as P

MESH = pl.DeviceIdType.MESH

TOK_DEV = 1536
CAP = 288
HD = 128
NY, NZ, NX = 4, 8, 4
WIDTH = 896
GROUP = 4
KAPPA = 128**-0.5 * 1.4426950408889634
NEG = -1e30
FILL = 64.0
TILE = 144
VROWS = 144
ALL_COLS = ((0, 384), (384, 384), (768, 384))
LOW_COLS = ((0, 384), (384, 256))
HIGH_COLS = ((640, 512),)

ROWS = {"A": 176, "B": 112}
FIRST = {"A": 0, "B": 176}
TURNS = {"A": (4, 3), "B0": (4, 3), "Bm": (3, 4), "Bp": (3, 4), "B2": (3, 4)}
ROW_OF = {"A": 0, "B0": 0, "Bm": 3, "Bp": 1, "B2": 2}
OFFSETS = (0, -1, -2, -3, 4, 1, 2, 3)
UPWARDS = (0, -1, -2, -3)
FIRST_SENDS = ("A", "YB", "YA", "B0")
UNITS = (
    (("ZR", "A", 1), ("ZL", "A", 1), ("YP", 0), ("YB", "P"), ("YB", "M"), ("ZR", "B0", 1), ("ZL", "B0", 1),),
    (("YM", 0), ("ZR", "A", 2), ("YM", -1), ("ZL", "A", 2),),
    (("YP", -1), ("YM", 1), ("YP", 1), ("YB", "2"), ("ZR", "B0", 2),),
    (("YP2", 0), ("ZR", "A", 3), ("YM", -2), ("ZL", "B0", 2), ("ZL", "Bm", 1),),
    (("ZL", "A", 3), ("YP", -2), ("YM", 2), ("ZR", "Bm", 1), ("ZR", "Bp", 1),),
    (("YP", 2), ("ZL", "Bp", 1), ("ZR", "B0", 3), ("ZL", "B0", 3), ("ZR", "B2", 1), ("ZL", "B2", 1),),
    (("YM2", 1), ("YP2", -1), ("YM", -3), ("ZL", "Bm", 2), ("ZL", "Bp", 2),),
    (("ZR", "A", 4), ("YP", -3), ("YM", 3), ("YP", 3), ("YM2", 2), ("ZR", "Bm", 2),),
    (("YP2", -2), ("YM", 4), ("ZL", "B2", 2), ("ZR", "Bp", 2), ("ZR", "B0", 4), ("ZL", "Bm", 3), ("ZR", "B2", 2), ("ZL", "Bp", 3),),
    (("YP", 4), ("YM2", 3), ("YP2", -3), ("ZR", "Bm", 3), ("ZL", "B2", 3),),
    (("YM2", 4), ("ZR", "Bp", 3), ("ZL", "Bm", 4), ("ZR", "B2", 3),),
    (("ZL", "Bp", 4), ("ZL", "B2", 4),),
)
ORDER = (
    ("c", "diag"), ("w", "YB", "P"), ("w", "YB", "M"), ("w", "ZR", "A", 1), ("w", "ZL", "A", 1),
    ("w", "YP", 0), ("w", "YM", 0), ("w", "ZR", "B0", 1), ("w", "ZL", "B0", 1), ("c", 0), ("w", "YB", "2"),
    ("w", "ZR", "A", 2), ("w", "YM", -1), ("w", "ZL", "A", 2), ("c", 1), ("w", "YP", -1), ("w", "ZR", "B0", 2),
    ("w", "ZL", "B0", 2), ("w", "YM", 1), ("w", "YP", 1), ("c", 2), ("w", "ZL", "Bm", 1), ("w", "YP2", 0),
    ("w", "ZR", "A", 3), ("w", "YM", -2), ("c", 3), ("w", "ZR", "Bm", 1), ("w", "ZL", "A", 3), ("w", "YP", -2),
    ("w", "YM", 2), ("w", "ZR", "Bp", 1), ("w", "ZL", "Bp", 1), ("c", 4), ("w", "ZR", "B0", 3),
    ("w", "ZL", "B0", 3), ("w", "YP", 2), ("w", "YM2", 1), ("w", "ZR", "B2", 1), ("w", "ZL", "B2", 1), ("c", 5),
    ("w", "YP2", -1), ("w", "YM", -3), ("w", "ZL", "Bm", 2), ("w", "ZR", "A", 4), ("w", "ZL", "Bp", 2), ("c", 6),
    ("w", "YP", -3), ("w", "YM", 3), ("w", "ZR", "Bm", 2), ("w", "ZL", "B2", 2), ("w", "ZR", "Bp", 2),
    ("w", "YP", 3), ("w", "YM2", 2), ("c", 7), ("w", "ZR", "B0", 4), ("w", "ZL", "Bm", 3), ("w", "YP2", -2),
    ("w", "YM", 4), ("w", "ZR", "B2", 2), ("w", "ZL", "Bp", 3), ("c", 8), ("w", "ZR", "Bm", 3),
    ("w", "ZL", "B2", 3), ("w", "YP", 4), ("w", "YM2", 3), ("w", "ZR", "Bp", 3), ("w", "YP2", -3), ("c", 9),
    ("w", "ZL", "Bm", 4), ("w", "ZR", "B2", 3), ("w", "YM2", 4), ("w", "ZL", "Bp", 4), ("c", 10),
    ("w", "ZL", "B2", 4), ("c", 11),
)
OPENS = {
    ("ZR", "A", 2): ("Bm",),
    ("ZL", "A", 2): ("Bp",),
    ("ZL", "B0", 2): ("B2",),
}

Z_IDS = [(side, s, i + 1) for s, (r, l) in TURNS.items() for side, n in (("ZR", r), ("ZL", l)) for i in range(n)]
Y_IDS = [(kind, o) for kind in ("YP", "YM") for o in OFFSETS]
Y_IDS += [("YP2", o) for o in UPWARDS] + [("YM2", o) for o in OFFSETS if o not in UPWARDS]
Y_IDS += [("YB", "P"), ("YB", "M"), ("YB", "2")]
G_IDS = Z_IDS + Y_IDS
N_GATHER = len(G_IDS)
NUMBER = {name: i for i, name in enumerate(G_IDS)}


def part_of(name):
    return "A" if name[1] == "A" or (name[0][0] == "Y" and name[0] != "YB") else "B"


PLACE, UNIT_ROWS = {}, []
for unit_pieces in UNITS:
    begin = sum(UNIT_ROWS)
    end = begin
    for piece in unit_pieces:
        PLACE[piece] = end
        end += ROWS[part_of(piece)]
    UNIT_ROWS.append(end - begin)

BLOCKS = (((0, 80), (80, 64)), ((144, 64), (208, 80)))


def kernel(
    q_hbm, k_ref, v_ref, picks_ref, router_ref, stream_hbm, w_hbm, out_hbm, q_ref, stream_ref, out_ref,
    own, held, stacked, vt, top, acc, w, att, sib_out, sib_in, hop_out, hop_in, end_out, end_in, total,
    send_sem, recv_sem, sib_send, sib_recv, x_send, x_recv, w_sem, in_sems, out_sems,
):
    ctx, ten = lax.axis_index("context"), lax.axis_index("tensor")
    y, z = ctx // NZ, lax.rem(ctx, NZ)
    x, core = ten // 2, lax.rem(ten, 2)

    def wrap(i, n):
        return lax.rem(i + 2 * n, n)

    def at_ctx(yy, zz):
        return (wrap(yy, NY) * NZ + wrap(zz, NZ), ten)

    def at_ten(xx, cc):
        return (ctx, wrap(xx, NX) * 2 + cc)

    up, down, right, left = at_ctx(y + 1, z), at_ctx(y - 1, z), at_ctx(y, z + 1), at_ctx(y, z - 1)
    sibling, x_up, x_down = at_ten(x, 1 - core), at_ten(x + 1, core), at_ten(x - 1, core)

    barrier = pltpu.get_barrier_semaphore()
    peers = (up, down, right, left, sibling, x_up, x_down)
    for peer in peers:
        pl.semaphore_signal(barrier, inc=1, device_id=peer, device_id_type=MESH)

    w_copy = pltpu.make_async_copy(w_hbm, w, w_sem)
    q_copy = pltpu.make_async_copy(q_hbm, q_ref, in_sems.at[0])
    stream_copy = pltpu.make_async_copy(stream_hbm, stream_ref, in_sems.at[1])
    q_copy.start()
    stream_copy.start()
    w_copy.start()

    picks = picks_ref[...].reshape(1, CAP)
    count = jnp.sum(jnp.where(picks < TOK_DEV, 1.0, 0.0), axis=1, keepdims=True)
    row_id = lax.broadcasted_iota(jnp.int32, (CAP, HD), 0)
    valid = row_id.astype(jnp.float32) < count
    k_all, v_all = k_ref[...], v_ref[...]
    own[:, :HD] = jnp.where(valid, k_all.astype(jnp.float32), k_all[:1].astype(jnp.float32)).astype(jnp.bfloat16)
    own[:, HD:] = jnp.where(valid, v_all.astype(jnp.float32), FILL).astype(jnp.bfloat16)

    def place(name):
        return held.at[pl.ds(PLACE[name], ROWS[part_of(name)]), :]

    def own_part(part):
        return own.at[pl.ds(FIRST[part], ROWS[part]), :]

    def own_row(offset):
        if offset == 0:
            return own_part("A")
        name = ("ZL", "A", offset) if 0 < offset < 4 else ("ZR", "A", -offset if offset < 0 else 4)
        return place(name)

    def source(name):
        kind = name[0]
        if kind in ("ZR", "ZL"):
            _, stream, step = name
            target = right if kind == "ZR" else left
            if step > 1:
                return place((kind, stream, step - 1)), target
            if stream in ("A", "B0"):
                return own_part(stream[0]), target
            return place(("YB", {"Bm": "P", "Bp": "M", "B2": "2"}[stream])), target
        if kind == "YB":
            return (place(("YB", "P")) if name[1] == "2" else own_part("B")), (down if name[1] == "M" else up)
        if kind == "YP":
            return own_row(name[1]), up
        if kind == "YM":
            return own_row(name[1]), down
        if kind == "YP2":
            return place(("YP", name[1])), up
        return place(("YM", name[1])), down

    def shard(name):
        kind = name[0]
        if kind in ("ZR", "ZL"):
            return wrap(y + ROW_OF[name[1]], NY), wrap(z - name[2] if kind == "ZR" else z + name[2], NZ)
        if kind == "YB":
            return wrap(y + {"P": -1, "M": 1, "2": 2}[name[1]], NY), z
        return wrap(y + {"YP": -1, "YM": 1, "YP2": 2, "YM2": 2}[kind], NY), wrap(z + name[1], NZ)

    def transfer(name):
        i = NUMBER[name]
        src, target = source(name)
        return pltpu.make_async_remote_copy(
            src, place(name), send_sem.at[i], recv_sem.at[i], device_id=target, device_id_type=MESH
        )

    def need(name, yy):
        kind = name[0]
        if kind in ("ZR", "ZL"):
            return {0: None, 3: yy >= 1, 1: yy == 3, 2: yy >= 2}[ROW_OF[name[1]]]
        if kind == "YB":
            return {"P": yy >= 1, "M": yy == 3, "2": yy >= 2}[name[1]]
        if kind == "YP":
            return yy >= 1
        if kind == "YM":
            return yy == 3 if name[1] in UPWARDS else jnp.logical_or(yy == 3, yy == 0)
        return yy >= 2

    def sent(name):
        if name[0] in ("ZR", "ZL"):
            return need(name, y)
        down_going = name[0] in ("YM", "YM2") or name == ("YB", "M")
        return need(name, wrap(y - 1 if down_going else y + 1, NY))

    def when(condition, action):
        if condition is None:
            action()
        else:

            @pl.when(condition)
            def _():
                action()

    def start(name):
        when(sent(name), transfer(name).start)

    def open_ring(stream):
        start(("ZR", stream, 1))
        start(("ZL", stream, 1))

    def open_column(offset):
        start(("YP", offset))
        start(("YM", offset))

    def arrive(name):
        kind = name[0]

        def receive():
            transfer(name).wait_recv()
            if kind in ("ZR", "ZL"):
                _, stream, step = name
                if step < TURNS[stream][0 if kind == "ZR" else 1]:
                    transfer((kind, stream, step + 1)).start()
            elif kind == "YP" and name[1] in UPWARDS:
                start(("YP2", name[1]))
            elif kind == "YM" and name[1] not in UPWARDS:
                start(("YM2", name[1]))
            elif name == ("YB", "P"):
                start(("YB", "2"))

        when(need(name, y), receive)
        if kind in ("ZR", "ZL") and name[1] == "A":
            open_column(name[2] if kind == "ZL" else (-name[2] if name[2] < 4 else 4))
        for stream in OPENS.get(name, ()):
            open_ring(stream)

    def tile(g, half):
        return pl.ds((half * GROUP + g) * TILE, TILE)

    def stack_queries():
        for half in (0, 1):
            for g in range(GROUP):
                stacked[tile(g, half), :] = q_ref[half * TILE : (half + 1) * TILE, g * HD : (g + 1) * HD]

    def qk(keys, cols):
        return lax.dot_general(
            keys, stacked[cols, :], (((1,), (1,)), ((), ())), preferred_element_type=jnp.float32
        )

    def diagonal():
        vt[:HD, :CAP] = jnp.transpose(v_ref[...])
        vt[HD:, :CAP] = jnp.ones((VROWS - HD, CAP), jnp.bfloat16)
        for first, width in ALL_COLS:
            cols = pl.ds(first, width)
            scores = qk(k_ref[...], cols)
            c = lax.broadcasted_iota(jnp.int32, (1, width), 1) + first
            i = jnp.where(c >= GROUP * TILE, TILE, 0) + lax.rem(c, TILE)
            j = lax.broadcasted_iota(jnp.int32, scores.shape, 0)
            scores = jnp.where(j <= i, scores, NEG)
            high = jnp.max(scores, axis=0, keepdims=True)
            weights = jnp.exp2((scores - high) * KAPPA).astype(jnp.bfloat16)
            acc[:, cols] = jnp.dot(vt[:, :CAP], weights, preferred_element_type=jnp.float32)
            top[:, cols] = jnp.broadcast_to(high, (8, width))

    def unit(u, columns=ALL_COLS, fill=True):
        n = UNIT_ROWS[u]
        here = pl.ds(PLACE[UNITS[u][0]], n)
        seen = []
        for name in UNITS[u]:
            yy, zz = shard(name)
            seen.append(jnp.logical_or(yy < y, jnp.logical_and(yy == y, zz < z)))
        some = seen[0]
        for other in seen[1:]:
            some = jnp.logical_or(some, other)

        @pl.when(some)
        def _():
            if fill:
                block = jnp.transpose(held[here, HD:])
                real = jnp.abs(block) < FILL / 2
                vt[:HD, :n] = jnp.where(real, block, 0).astype(jnp.bfloat16)
                vt[HD:, :n] = jnp.where(real[: VROWS - HD], 1, 0).astype(jnp.bfloat16)

            def score(cols):
                raw = qk(held[here, :HD], cols)
                parts, first = [], 0
                for name, shown in zip(UNITS[u], seen):
                    rows = ROWS[part_of(name)]
                    parts.append(jnp.where(shown, raw[first : first + rows], NEG))
                    first += rows
                return jnp.concatenate(parts, axis=0)

            def soften(cols, scores):
                old = top[:, cols]
                new = jnp.maximum(old, jnp.max(scores, axis=0, keepdims=True))
                top[:, cols] = new
                return jnp.exp2((scores - new[:1]) * KAPPA).astype(jnp.bfloat16), jnp.exp2((old - new) * KAPPA)

            def mix(cols, weights, factor):
                more = jnp.dot(vt[:, :n], weights, preferred_element_type=jnp.float32)
                acc[:, cols] = acc[:, cols] * factor[:1] + more

            spans = [pl.ds(*span) for span in columns]
            scores, waiting = score(spans[0]), None
            for at, cols in enumerate(spans):
                following = score(spans[at + 1]) if at + 1 < len(spans) else None
                softened = soften(cols, scores)
                if waiting is not None:
                    mix(*waiting)
                waiting, scores = (cols, *softened), following
            mix(*waiting)

    def normalize(half):
        first, width = ((0, 640), (512, 640))[half]
        cols = pl.ds(first, width)
        flat = jnp.transpose(acc[:HD, cols] / acc[HD : HD + 1, cols]).astype(jnp.bfloat16)
        for g in range(GROUP):
            start_row = (half * GROUP + g) * TILE - first
            att[half * TILE : (half + 1) * TILE, g * HD : (g + 1) * HD] = flat[start_row : start_row + TILE]

    def block_rows(b):
        return pl.ds(b * TILE, TILE)

    def partial(d, cc, b):
        cols = pl.ds(pl.multiple_of((wrap(x + d, NX) * 2 + cc) * WIDTH, 128), WIDTH)
        return jnp.dot(att[block_rows(b), :], w[:, cols], preferred_element_type=jnp.float32)

    def to_sibling(d, b):
        i = 2 * d + b
        return pltpu.make_async_remote_copy(
            sib_out.at[d, block_rows(b)], sib_in.at[d, block_rows(b)], sib_send.at[i], sib_recv.at[i],
            device_id=sibling, device_id_type=MESH,
        )

    def x_copy(kind, way, b):
        i = (kind * 2 + way) * 2 + b
        first, count_rows = BLOCKS[b][way if kind < 2 else 1 - way]
        rows = pl.ds(first, count_rows)
        if kind == 0:
            src, dst = hop_out.at[rows], hop_in.at[rows]
        else:
            src, dst = end_out.at[way, rows], end_in.at[way, rows]
        return pltpu.make_async_remote_copy(
            src, dst, x_send.at[i], x_recv.at[i], device_id=(x_up, x_down)[way], device_id_type=MESH
        )

    def send_sibling(d, b):
        sib_out[d, block_rows(b)] = partial(d, 1 - core, b).astype(jnp.bfloat16)
        to_sibling(d, b).start()

    def chip_sum(d, b):
        mine = partial(d, core, b)
        to_sibling(d, b).wait_recv()
        return mine + sib_in[d, block_rows(b)].astype(jnp.float32)

    def far(b):
        send_sibling(2, b)
        send_sibling(1, b)
        hop_out[block_rows(b), :] = chip_sum(2, b).astype(jnp.bfloat16)
        x_copy(0, 0, b).start()
        x_copy(0, 1, b).start()
        send_sibling(3, b)

    def near(b):
        for way, d in ((0, 1), (1, 3)):
            total[way, block_rows(b)] = chip_sum(d, b)
            first, count_rows = BLOCKS[b][1 - way]
            rows = pl.ds(first, count_rows)
            end_out[way, rows] = total[way, rows].astype(jnp.bfloat16)
            x_copy(2, way, b).start()
        send_sibling(0, b)

    def pass_on(b):
        for way in (0, 1):
            first, count_rows = BLOCKS[b][way]
            rows = pl.ds(first, count_rows)
            x_copy(0, way, b).wait_recv()
            end_out[way, rows] = (total[way, rows] + hop_in[rows, :].astype(jnp.float32)).astype(jnp.bfloat16)
            x_copy(1, way, b).start()

    def out_copy(b, way):
        here = pl.ds(*BLOCKS[b][way])
        return pltpu.make_async_copy(out_ref.at[here], out_hbm.at[here], out_sems.at[2 * b + way])

    def finish(b):
        rows = block_rows(b)
        total[0, rows] = chip_sum(0, b)
        for way in (0, 1):
            here = pl.ds(*BLOCKS[b][way])
            x_copy(2, 1 - way, b).wait_recv()
            x_copy(1, way, b).wait_recv()
            projected = total[0, here] + end_in[0, here].astype(jnp.float32) + end_in[1, here].astype(jnp.float32)
            residual = stream_ref[here, :].astype(jnp.float32)
            inside = slice(BLOCKS[b][way][0], sum(BLOCKS[b][way]))
            updated = jnp.where(wide_valid[inside], residual + gain[inside] * projected, residual)
            out_ref[here, :] = updated.astype(jnp.bfloat16)
            out_copy(b, way).start()

    q_copy.wait()
    stack_queries()
    pl.semaphore_wait(barrier, len(peers))
    for what in FIRST_SENDS:
        if what == "YB":
            start(("YB", "P"))
            start(("YB", "M"))
        elif what == "YA":
            open_column(0)
        else:
            open_ring(what)

    for what, *rest in ORDER[:-1]:
        if what == "w":
            arrive(tuple(rest))
        elif rest[0] == "diag":
            diagonal()
        else:
            unit(rest[0])

    unit(ORDER[-1][1], LOW_COLS)
    normalize(0)
    w_copy.wait()
    far(0)
    unit(ORDER[-1][1], HIGH_COLS, False)
    normalize(1)
    near(0)
    far(1)
    pass_on(0)
    near(1)
    pass_on(1)

    router = router_ref[...].reshape(1, CAP)
    eye = lax.broadcasted_iota(jnp.int32, (CAP, CAP), 0) == lax.broadcasted_iota(jnp.int32, (CAP, CAP), 1)
    gain = jnp.sum(jnp.where(eye, router, 0.0), axis=1, keepdims=True)
    wide_valid = lax.broadcasted_iota(jnp.int32, (CAP, WIDTH), 0).astype(jnp.float32) < count
    for name in G_IDS:
        when(sent(name), transfer(name).wait_send)
    for b in (0, 1):
        for d in range(NX):
            to_sibling(d, b).wait_send()
    stream_copy.wait()
    finish(0)
    finish(1)
    for b in (0, 1):
        for way in (0, 1):
            out_copy(b, way).wait()
    for b in (0, 1):
        for kind in range(3):
            for way in (0, 1):
                x_copy(kind, way, b).wait_send()


def local(stream_rows, picks, router, queries, keys, values, out_weight):
    vmem, anywhere = pl.BlockSpec(memory_space=pltpu.VMEM), pl.BlockSpec(memory_space=pl.ANY)
    bf16, f32 = jnp.bfloat16, jnp.float32
    dma = pltpu.SemaphoreType.DMA
    return pl.pallas_call(
        kernel,
        out_shape=jax.ShapeDtypeStruct(stream_rows.shape, bf16),
        in_specs=[anywhere] + [vmem] * 4 + [anywhere] * 2,
        out_specs=anywhere,
        scratch_shapes=[
            pltpu.VMEM(queries.shape, bf16),
            pltpu.VMEM(stream_rows.shape, bf16),
            pltpu.VMEM(stream_rows.shape, bf16),
            pltpu.VMEM((CAP, 2 * HD), bf16),
            pltpu.VMEM((sum(UNIT_ROWS), 2 * HD), bf16),
            pltpu.VMEM((GROUP * CAP, HD), bf16),
            pltpu.VMEM((VROWS, max(UNIT_ROWS)), bf16),
            pltpu.VMEM((8, GROUP * CAP), f32),
            pltpu.VMEM((VROWS, GROUP * CAP), f32),
            pltpu.VMEM(out_weight.shape, bf16),
            pltpu.VMEM((CAP, GROUP * HD), bf16),
            pltpu.VMEM((NX, CAP, WIDTH), bf16),
            pltpu.VMEM((NX, CAP, WIDTH), bf16),
            pltpu.VMEM((CAP, WIDTH), bf16),
            pltpu.VMEM((CAP, WIDTH), bf16),
            pltpu.VMEM((2, CAP, WIDTH), bf16),
            pltpu.VMEM((2, CAP, WIDTH), bf16),
            pltpu.VMEM((2, CAP, WIDTH), f32),
            dma((N_GATHER,)),
            dma((N_GATHER,)),
            dma((2 * NX,)),
            dma((2 * NX,)),
            dma((12,)),
            dma((12,)),
            dma,
            dma((2,)),
            dma((4,)),
        ],
        compiler_params=pltpu.CompilerParams(
            collective_id=0, has_side_effects=True, vmem_limit_bytes=56 * 2**20
        ),
        cost_estimate=pl.CostEstimate(flops=8 * 10**9, bytes_accessed=10**7, transcendentals=10**7),
    )(queries, keys, values, picks, router, stream_rows, out_weight)


def solution(mesh):
    placed = (
        P("context", "tensor"),
        P("context"),
        P("context"),
        P("context", "tensor"),
        P("context", "tensor"),
        P("context", "tensor"),
        P("tensor", None),
    )
    return jax.shard_map(
        local, mesh=mesh, in_specs=placed, out_specs=P("context", "tensor"), check_vma=False
    )
```
